32 devices in a mesh: blk: 2 (over y), dp: 16 (over z, x, core).
Axes of the slice: x: 2, y: 2, z: 4, core: 2. Of those that a mesh axis runs over, the one named last changes fastest.
Arguments:
- tokens: bfloat16 [16, 454, 768], P('dp', 'blk'), may hold values from -6 to 6
- segment_ids: int32 [16, 454], P('dp'), may hold values from 0 to 5, as said below
- expert_ids: int32 [16, 454], P('dp'), may hold values from 0 to 2, as said below
- norm_first: float32 [768], replicated, may hold values from 0.5 to 1.5
- project_in: bfloat16 [768, 2304], replicated, may hold values from -0.21875 to 0.21875
- project_out: bfloat16 [768, 768], replicated, may hold values from -2 to 2
- norm_second: float32 [768], replicated, may hold values from 0.5 to 1.5
- up_weight: bfloat16 [3, 768, 3072], P(None, None, 'blk'), may hold values from -0.21875 to 0.21875
- down_weight: bfloat16 [3, 3072, 768], P(None, 'blk'), may hold values from -0.109375 to 0.109375
- cotangent: bfloat16 [16, 454, 768], P('dp', 'blk'), may hold values from -6 to 6
Outputs:
- layer_out: bfloat16 [16, 454, 768], P('dp', 'blk')
- input_grad: bfloat16 [16, 454, 768], P('dp', 'blk')
- grad_norm_first: float32 [768], P('dp')
- grad_project_in: float32 [768, 2304], P('dp')
- grad_project_out: float32 [768, 768], P('dp')
- grad_norm_second: float32 [768], P('dp')
- grad_up: float32 [3, 768, 3072], P(None, 'dp', 'blk')
- grad_down: float32 [3, 3072, 768], P(None, 'blk', 'dp')
The draws below stay inside these ranges and needn't reach their ends.
Inputs may be any that keep to these rules, and one draw needn't show every extreme that they name: `segment_ids`: each group holds some whole captions numbered 1 upward, then its 197 image tokens (id 0), which take the last slots of the first 227 and the first slots of the rest, then its remaining captions numbered on; every caption has 1 to 64 tokens and caption 1 has 64. `expert_ids`: the same for all tokens of one image or one caption; an image's tokens use expert 0 or 2, a caption's expert 1 or 2.
All inputs are finite; a program needn't handle non-finite values.
Results may differ from the reference program's by a relative error of at most 0.015.
Values may be sent and summed in bfloat16 or wider, within the bound.
No kernel may reach another device: no remote copies, remote signals or barrier semaphores. Data moves between devices by JAX's collectives and lax.ppermute only.
A program may use at most 256 MiB of HBM per device.

```python
import jax
import jax.numpy as jnp
from jax import lax

D = 768
HEADS = 12
HEAD_DIM = 64
FF = 3072
EXPERTS = 3
PATCHES = 197
CAPTION = 64
CAPS = 5
SLOTS = 454
PACKS = 16


def pack_layout(key):
    layout_key = jax.random.fold_in(key, 101)
    half = SLOTS // 2
    lowest = max(half - PATCHES + 1, CAPTION + 1)
    highest = half - 1
    before = jax.random.randint(layout_key, (PACKS,), lowest, highest + 1).astype(jnp.int32)
    first_count = (before + CAPTION - 1) // CAPTION
    rest_count = CAPS - first_count
    after = SLOTS - PATCHES - before
    base_len = jnp.maximum(after // rest_count, 1)
    extra = after % rest_count
    slot_index = jnp.arange(SLOTS, dtype=jnp.int32)[None, :]
    before_col = before[:, None]
    front = slot_index // CAPTION + 1
    tail = slot_index - before_col - PATCHES
    long_part = extra[:, None] * (base_len[:, None] + 1)
    tail_index = jnp.where(tail < long_part, tail // (base_len[:, None] + 1), extra[:, None] + (tail - long_part) // base_len[:, None])
    back = first_count[:, None] + 1 + tail_index
    segment = jnp.where(slot_index < before_col, front, jnp.where(tail < 0, 0, back))
    return segment.astype(jnp.int32)


def draw_segment_ids(key, part):
    return pack_layout(key)


def draw_expert_ids(key, part):
    segment = pack_layout(key)
    key = jax.random.fold_in(key, 7)
    coins = jax.random.randint(key, (PACKS, CAPS + 1), 0, 3)
    coins = coins.at[0, 0].set(0)
    coins = coins.at[0, 1].set(1)
    coins = coins.at[1, 0].set(1)
    chosen = jnp.take_along_axis(coins, segment, axis=1)
    modality = (segment > 0).astype(jnp.int32)
    return jnp.where(chosen == 0, EXPERTS - 1, modality).astype(jnp.int32)


def levels(key, extent, cuts, low, top_value):
    factor_of, own = 1.0, jax.random.fold_in(key, 6)
    for axis_at, shards_of in cuts:
        heights = jnp.exp(jax.random.uniform(jax.random.fold_in(own, axis_at), (shards_of,), jnp.float32, low / len(cuts), top_value / len(cuts)))
        factor_of = factor_of * jnp.repeat(heights, extent[axis_at] // shards_of).reshape([-1 if axis == axis_at else 1 for axis in range(len(extent))])
    return factor_of


def normal_values(key, shape, width, reach, pieces=(), held_as=jnp.bfloat16):
    factor_of = levels(key, shape, pieces, -0.22, 0.18) if pieces else 1.0
    array = jax.random.normal(key, shape, jnp.float32) * width * factor_of
    return jnp.minimum(jnp.maximum(array, -reach), reach).astype(held_as)


def setup_inputs(seed: int = 0) -> dict:
    keys = jax.random.split(jax.random.key(seed), 11)
    tokens = normal_values(keys[0], (PACKS, SLOTS, D), 1.0, 6.0, ((0, 16), (1, 2)))
    segment_ids = draw_segment_ids(jax.random.fold_in(keys[10], 71), 0)
    expert_ids = draw_expert_ids(jax.random.fold_in(keys[10], 71), 0)
    norm_first = jnp.clip(1.0 + 0.1 * jax.random.normal(keys[3], (D,), jnp.float32), 0.5, 1.5)
    project_in = normal_values(keys[4], (D, 3 * D), D ** -0.5, 0.21875)
    project_out = normal_values(keys[5], (D, D), 8 ** -0.5, 2.0)
    norm_second = jnp.clip(1.0 + 0.1 * jax.random.normal(keys[6], (D,), jnp.float32), 0.5, 1.5)
    up_weight = normal_values(keys[7], (EXPERTS, D, FF), D ** -0.5, 0.21875, ((2, 2),))
    down_weight = normal_values(keys[8], (EXPERTS, FF, D), FF ** -0.5, 0.109375, ((1, 2),))
    cotangent = normal_values(keys[9], (PACKS, SLOTS, D), 1.0, 6.0, ((0, 16), (1, 2)))
    return dict(tokens=tokens, segment_ids=segment_ids, expert_ids=expert_ids, norm_first=norm_first, project_in=project_in, project_out=project_out, norm_second=norm_second, up_weight=up_weight, down_weight=down_weight, cotangent=cotangent)


EPSILON = 1e-05
NEGATIVE = -1e+30
HIGHEST = lax.Precision.HIGHEST
ROOT_HALF = 0.7071067811865476

@jax.custom_vjp
def low(v):
    return lax.optimization_barrier(v.astype(jnp.bfloat16)).astype(jnp.float32)

@jax.custom_vjp
def low_back(v):
    return v

def low_keep(v):
    return (low(v), None)

def low_pass(kept, grad):
    return (grad,)

def back_keep(v):
    return (v, None)

def back_low(kept, grad):
    return (low(grad),)
low.defvjp(low_keep, low_pass)
low_back.defvjp(back_keep, back_low)

def layer_norm(values, gain):
    row_mean = lax.optimization_barrier(jnp.mean(values, axis=-1, keepdims=True))
    centred = values - row_mean
    row_var = lax.optimization_barrier(jnp.mean(centred * centred, axis=-1, keepdims=True))
    return centred * lax.rsqrt(row_var + EPSILON) * gain

def gelu_value(upward):
    return 0.5 * upward * (1.0 + lax.erf(upward * ROOT_HALF))

def pack_layer(pack_rows, segment_row, expert_row, norm_one, weight_in, weight_out, norm_two, weight_up, weight_down):
    row_count = pack_rows.shape[0]
    normed = low(layer_norm(pack_rows, norm_one))
    projected = jnp.dot(normed, weight_in, precision=HIGHEST)
    queries = low(low_back(projected[:, :D])).reshape(row_count, HEADS, HEAD_DIM)
    key_rows = low(low_back(projected[:, D:2 * D])).reshape(row_count, HEADS, HEAD_DIM)
    value_rows = low(low_back(projected[:, 2 * D:])).reshape(row_count, HEADS, HEAD_DIM)
    scores = low_back(jnp.einsum('qhd,khd->hqk', queries, key_rows, precision=HIGHEST) * HEAD_DIM ** (-0.5))
    allowed = (segment_row[None, :] == 0) | (segment_row[None, :] == segment_row[:, None])
    scores = jnp.where(allowed[None], scores, NEGATIVE)
    row_peak = lax.optimization_barrier(jnp.max(scores, axis=-1, keepdims=True))
    raised = jnp.exp(scores - row_peak)
    probs = low(raised / lax.optimization_barrier(jnp.sum(raised, axis=-1, keepdims=True)))
    heads_out = jnp.einsum('hqk,khd->qhd', probs, value_rows, precision=HIGHEST).reshape(row_count, D)
    attended = low(low_back(heads_out))
    branch = low_back(jnp.dot(attended, weight_out, precision=HIGHEST))
    middle = pack_rows + branch
    normed_two = low(layer_norm(middle, norm_two))
    onehot = (expert_row[:, None] == jnp.arange(EXPERTS, dtype=jnp.int32)[None, :]).astype(jnp.float32)
    summed = jnp.zeros_like(middle)
    for expert_index in range(EXPERTS):
        upward = low_back(jnp.dot(normed_two, weight_up[expert_index], precision=HIGHEST))
        active = low(gelu_value(upward))
        summed = summed + onehot[:, expert_index:expert_index + 1] * jnp.dot(active, weight_down[expert_index], precision=HIGHEST)
    return middle + low_back(summed)

def reference(tokens, segment_ids, expert_ids, norm_first, project_in, project_out, norm_second, up_weight, down_weight, cotangent):

    def forward_all(rows_all, norm_one, weight_in, weight_out, norm_two, weight_up, weight_down):

        def one_pack(pack_item):
            pack_rows, segment_row, expert_row = pack_item
            return pack_layer(pack_rows, segment_row, expert_row, norm_one, weight_in, weight_out, norm_two, weight_up, weight_down)
        return lax.map(jax.checkpoint(one_pack), (rows_all, segment_ids, expert_ids))
    floats = (tokens.astype(jnp.float32), norm_first.astype(jnp.float32), project_in.astype(jnp.float32), project_out.astype(jnp.float32), norm_second.astype(jnp.float32), up_weight.astype(jnp.float32), down_weight.astype(jnp.float32))
    outputs, pullback = jax.vjp(forward_all, *floats)
    gradients = pullback(cotangent.astype(jnp.float32))
    return (outputs.astype(jnp.bfloat16), gradients[0].astype(jnp.bfloat16), gradients[1], gradients[2], gradients[3], gradients[4], gradients[5], gradients[6])
```

```python
import functools

import jax
import jax.numpy as jnp
import numpy as np
from jax import lax
from jax.experimental import pallas as pl
from jax.experimental.pallas import tpu as pltpu
from jax.sharding import PartitionSpec as P

HEADS = 12
HEAD_DIM = 64
EXPERTS = 3
EPSILON = 1e-05
NEGATIVE = -1e30
ROOT_HALF = 0.7071067811865476
INV_ROOT_TAU = 0.3989422804014327
SCALE = HEAD_DIM ** (-0.5)
LOG2_E = 1.4426950408889634
LANES = 128
INNER = 16
CORE, NEAR, MID, FAR = 1, 2, 4, 8

f32 = jnp.float32
bf16 = jnp.bfloat16

NN = ((1,), (0,))
NT = ((1,), (1,))
TN = ((0,), (0,))


def across_blk(value):
    return lax.ppermute(value, "blk", [(0, 1), (1, 0)])


def across_dp(value, bit):
    count = lax.axis_size("dp")
    return lax.ppermute(value, "dp", [(source, source ^ bit) for source in range(count)])


def after(value, *others):
    return lax.optimization_barrier((value, others))[0]


def dot(a, b, dims=NN):
    return lax.dot_general(a, b, (dims, ((), ())), preferred_element_type=f32)


def layer_norm_parts(values):
    row_mean = jnp.mean(values, axis=-1, keepdims=True)
    centred = values - row_mean
    row_var = jnp.mean(centred * centred, axis=-1, keepdims=True)
    scale = lax.rsqrt(row_var + EPSILON)
    return centred * scale, scale


def layer_norm_back(grad, gain, unit, scale):
    raised = grad * gain
    return scale * (
        raised
        - jnp.mean(raised, axis=-1, keepdims=True)
        - unit * jnp.mean(raised * unit, axis=-1, keepdims=True)
    )


def whole():
    return pl.BlockSpec(memory_space=pltpu.VMEM)


def scalars():
    return pl.BlockSpec(memory_space=pltpu.SMEM)


def shaped(shape, dtype):
    return jax.ShapeDtypeStruct(shape, dtype)


def held(shape, dtype):
    size = np.dtype(dtype).itemsize
    lead = int(np.prod(shape[:-2])) if len(shape) > 2 else 1
    deep = shape[-2] if len(shape) > 1 else 1
    return lead * -(-deep // 16) * 16 * -(-shape[-1] // LANES) * LANES * size


def call(kernel, name, out_shape, scratch=(), flops=0, small=0, room=4, aliases=None):
    def run(*operands):
        outs = out_shape if isinstance(out_shape, list) else [out_shape]
        moved = sum(held(a.shape, a.dtype) for a in operands[small:]) + sum(
            held(o.shape, o.dtype) for o in outs
        )
        need = moved + sum(held(v.shape, v.dtype) for v in scratch) + room * 2**20
        return pl.pallas_call(
            kernel,
            name=name,
            out_shape=out_shape,
            in_specs=[scalars()] * small + [whole()] * (len(operands) - small),
            out_specs=[whole()] * len(outs) if isinstance(out_shape, list) else whole(),
            scratch_shapes=list(scratch),
            input_output_aliases=aliases or {},
            compiler_params=pltpu.CompilerParams(vmem_limit_bytes=need),
            cost_estimate=pl.CostEstimate(flops=flops, bytes_accessed=moved, transcendentals=0),
        )(*operands)

    return run


def begin_kernel(
    count, deep, outer, place, side, ids, experts, own, gain, w_in,
    seg_col, seg_row, hot, hot_row, order, projected, normed_ref, token_rows,
):
    rows = seg_col.shape[0]
    span, width = rows // 2, own.shape[1]
    on_side = side[0] == 0

    def both(values):
        halves = values[0:1, :count], values[0:1, count:]
        pad = jnp.full((1, span - count), -1, jnp.int32)
        first = jnp.where(on_side, halves[0], halves[1])
        second = jnp.where(on_side, halves[1], halves[0])
        return jnp.broadcast_to(jnp.concatenate([first, pad, second, pad], axis=1), (8, rows))

    segments, expert = both(ids), both(experts)
    seg_row[...] = segments
    seg_col[...] = jnp.transpose(segments).astype(jnp.int32)
    kinds = lax.broadcasted_iota(jnp.int32, (8, rows), 0)
    hot_row[...] = (kinds == expert).astype(f32)
    turned = jnp.transpose(expert)
    hot[...] = (lax.broadcasted_iota(jnp.int32, (rows, 8), 1) == turned).astype(bf16)
    step = outer * deep
    lane = lax.broadcasted_iota(jnp.int32, (step, width), 1)
    low = lax.broadcasted_iota(jnp.int32, (step, width), 0)
    skip = low
    for late in range(1, outer):
        skip += jnp.where(low >= late * deep, (INNER - 1) * deep, 0)
    for block in range(INNER // 2):
        relative = ((block >> 2) & 1) * NEAR + ((block >> 1) & 1) * MID + (block & 1) * FAR
        base = (place[0] ^ relative) * deep
        order[block * step : (block + 1) * step, :] = (lane - base == skip).astype(f32).astype(bf16)
    token_rows[...] = jnp.zeros_like(token_rows)
    token_rows[0:count, :] = own[...].astype(f32)
    unit, _ = layer_norm_parts(token_rows[...])
    normed = (unit * gain[...]).astype(bf16)
    normed_ref[...] = normed
    projected[0:span, :] = dot(normed, w_in[...]).astype(bf16)


def begin(place, side, ids, experts, own, gain, w_in, deep, outer):
    count, width = own.shape
    span = -(-count // LANES) * LANES
    rows = 2 * span
    return call(
        functools.partial(begin_kernel, count, deep, outer),
        "begin",
        [
            shaped((rows, 8), jnp.int32),
            shaped((8, rows), jnp.int32),
            shaped((rows, 8), bf16),
            shaped((8, rows), f32),
            shaped((width // 2, width), bf16),
            shaped((rows, 3 * width), bf16),
            shaped((span, width), bf16),
            shaped((span, width), f32),
        ],
        flops=span * width * width * 6,
        small=2,
    )(place, side, ids, experts, own, gain, w_in)


def front_kernel(
    own_rows, own_normed, far, seg_col, seg_row, gain_one, gain_two, w_in, w_out, half_done,
    projected, packed, middle_ref, token_rows, lse_ref, bias,
):
    count, width = far.shape
    rows = projected.shape[0]
    span = rows // 2
    token_rows[0:span, :] = own_rows[...]
    token_rows[span:, :] = jnp.zeros((span, width), f32)
    token_rows[span : span + count, :] = far[...].astype(f32)
    unit, _ = layer_norm_parts(token_rows[span:, :])
    normed = (unit * gain_one[...]).astype(bf16)
    packed[1, :span, :] = own_normed[...]
    packed[1, span:, :] = normed
    projected[:span, :] = half_done[:span, :]
    projected[span:, :] = dot(normed, w_in[...]).astype(bf16)
    allowed = (seg_row[0:1, :] == 0) | (seg_row[0:1, :] == seg_col[:, 0:1])
    bias[...] = jnp.where(allowed, 0.0, NEGATIVE)
    lane = lax.broadcasted_iota(jnp.int32, (rows, LANES), 1)
    first = lane < HEAD_DIM
    lse_ref[...] = jnp.zeros_like(lse_ref)

    def pair(p, _):
        def columns(shift):
            return pl.ds(pl.multiple_of(shift + p * LANES, LANES), LANES)

        queries = projected[:, columns(0)] * jnp.asarray(SCALE, bf16)
        keys = projected[:, columns(width)]
        values = projected[:, columns(2 * width)]
        outs = []
        for head in range(2):
            mine = first if head == 0 else jnp.logical_not(first)
            scores = dot(jnp.where(mine, queries, jnp.zeros_like(queries)), keys, NT)
            scores = scores * LOG2_E + bias[...]
            peak = jnp.max(scores, axis=-1, keepdims=True)
            raised = jnp.exp2(scores - peak).astype(bf16)
            summed = dot(raised, jnp.where(mine, values, jnp.ones_like(values)))
            at = (1 - head) * HEAD_DIM
            total = summed[:, at : at + 1]
            outs.append(summed / total)
            lse_ref[...] = jnp.where(lane == 2 * p + head, peak + jnp.log2(total), lse_ref[...])
        packed[2, :, columns(0)] = jnp.where(first, outs[0], outs[1]).astype(bf16)
        return 0

    lax.fori_loop(0, width // LANES, pair, 0)
    middle = token_rows[...] + dot(packed[2], w_out[...])
    middle_ref[...] = middle
    unit, _ = layer_norm_parts(middle)
    packed[0] = (unit * gain_two[...]).astype(bf16)


def front(own_rows, own_normed, far, seg_col, seg_row, gain_one, gain_two, w_in, w_out, half_done):
    rows, three = half_done.shape
    width = three // 3
    return call(
        front_kernel,
        "front",
        [
            shaped((rows, three), bf16),
            shaped((3, rows, width), bf16),
            shaped((rows, width), f32),
            shaped((rows, width), f32),
            shaped((rows, LANES), f32),
        ],
        scratch=[pltpu.VMEM((rows, rows), f32)],
        flops=6_000_000_000,
        room=8,
    )(own_rows, own_normed, far, seg_col, seg_row, gain_one, gain_two, w_in, w_out, half_done)


def masked_rows(target, value, hot):
    span = value.shape[1]
    for e in range(EXPERTS):
        target[:, e * span : (e + 1) * span] = value * hot[:, e : e + 1]


def up_kernel(packed, hot, hot_row, own_grads, far_grads, weight, active_ref, slope_ref, message, masked):
    width, hidden = packed.shape[2], weight.shape[2]
    rows = packed.shape[1]
    masked_rows(masked, packed[0], hot)
    count, span = own_grads.shape[0], rows // 2
    message[...] = jnp.zeros_like(message)
    message[0:count, :] = own_grads[...]
    message[span : span + count, :] = far_grads[...]
    message[rows : rows + 8, :rows] = hot_row[...].astype(bf16)
    chunk = 512
    for n in range(0, hidden, chunk):
        upward = dot(
            masked[...], weight[:, :, n : n + chunk].reshape(EXPERTS * width, chunk)
        )
        half = 0.5 * (1.0 + lax.erf(upward * ROOT_HALF))
        active_ref[:, n : n + chunk] = (upward * half).astype(bf16)
        slope_ref[:, n : n + chunk] = half + upward * INV_ROOT_TAU * jnp.exp(-0.5 * upward * upward)


def up_forward(packed, hot, hot_row, own_grads, far_grads, up_weight):
    _, rows, width = packed.shape
    hidden = up_weight.shape[2]
    return call(
        up_kernel,
        "up_forward",
        [
            shaped((rows, hidden), bf16),
            shaped((rows, hidden), f32),
            shaped((rows + 16, width), bf16),
        ],
        scratch=[pltpu.VMEM((rows, EXPERTS * width), bf16)],
        flops=2 * rows * width * hidden * EXPERTS,
        room=6,
    )(packed, hot, hot_row, own_grads, far_grads, up_weight)


def grad_upward_kernel(message, hot, weight, slope, out_ref, masked):
    rows, hidden = out_ref.shape
    width = message.shape[1]
    masked_rows(masked, message[:rows, :], hot)
    chunk = 512
    for n in range(0, hidden, chunk):
        total = dot(masked[:, :width], weight[0, n : n + chunk, :], NT)
        for e in range(1, EXPERTS):
            total += dot(masked[:, e * width : (e + 1) * width], weight[e, n : n + chunk, :], NT)
        out_ref[:, n : n + chunk] = (total * slope[:, n : n + chunk]).astype(bf16)


def grad_upward_of(message, hot, down_weight, slope):
    rows, width = slope.shape[0], message.shape[1]
    hidden = down_weight.shape[1]
    return call(
        grad_upward_kernel,
        "grad_upward",
        shaped((rows, hidden), bf16),
        scratch=[pltpu.VMEM((rows, EXPERTS * width), bf16)],
        flops=2 * rows * width * hidden * EXPERTS,
        room=6,
    )(message, hot, down_weight, slope)


def hidden_back_kernel(dims, rows_ref, hot, weight, out_ref, masked):
    hidden, width = rows_ref.shape[1], out_ref.shape[1]
    masked_rows(masked, rows_ref[...], hot)
    chunk = 256
    for n in range(0, width, chunk):
        total = jnp.zeros((rows_ref.shape[0], chunk), f32)
        for e in range(EXPERTS):
            part = weight[e, n : n + chunk, :] if dims is NT else weight[e, :, n : n + chunk]
            total += dot(masked[:, e * hidden : (e + 1) * hidden], part, dims)
        out_ref[:, n : n + chunk] = total.astype(out_ref.dtype)


def hidden_back(dims, name, rows_ref, hot, weight):
    rows, hidden = rows_ref.shape
    width = weight.shape[1] if dims is NT else weight.shape[2]
    return call(
        functools.partial(hidden_back_kernel, dims),
        name,
        shaped((rows, width), bf16),
        scratch=[pltpu.VMEM((rows, EXPERTS * hidden), bf16)],
        flops=2 * rows * width * hidden * EXPERTS,
        room=6,
    )(rows_ref, hot, weight)


def picked_kernel(order, hot_own, hot_far, own, far, own_ref, far_ref):
    rows = own_ref.shape[2]
    for source, hot, target in ((own, hot_own, own_ref), (far, hot_far, far_ref)):
        values = source[0] if len(source.shape) == 3 else source[:rows, :]
        turned = dot(order[...], values, NT)
        for e in range(EXPERTS):
            target[e] = (turned * hot[e : e + 1, :rows].astype(f32)).astype(bf16)


def picked(order, hot_own, hot_far, own, far):
    rows = hot_own.shape[1]
    shape = shaped((EXPERTS, order.shape[0], rows), bf16)
    return call(
        picked_kernel,
        "picked",
        [shape, shape],
        flops=4 * order.shape[0] * order.shape[1] * rows,
    )(order, hot_own, hot_far, own, far)


def expert_grad_kernel(expert, a_own, a_far, b_own, b_far, keep_ref, send_ref):
    half = keep_ref.shape[0]
    chunk = 512
    for n in range(0, b_own.shape[1], chunk):
        both = dot(a_own[expert], b_own[:, n : n + chunk])
        both += dot(a_far[expert], b_far[:, n : n + chunk])
        keep_ref[:, n : n + chunk] = both[:half].astype(bf16)
        send_ref[:, n : n + chunk] = both[half:].astype(bf16)


def expert_grad(expert, a_own, a_far, b_own, b_far):
    _, wide, rows = a_own.shape
    hidden = b_own.shape[1]
    shape = shaped((wide // 2, hidden), bf16)
    return call(
        functools.partial(expert_grad_kernel, expert),
        "expert_grad",
        [shape, shape],
        flops=4 * wide * rows * hidden,
    )(a_own, a_far, b_own, b_far)


def attention_grad_kernel(order, own, far, g_own, g_far, keep_ref, send_ref):
    half = keep_ref.shape[0]
    rows, span = own.shape[1], g_own.shape[1]
    for plane, blocks in ((1, (0, 1, 2)), (2, (3,))):
        near = dot(order[...], own[plane], NT).astype(bf16)
        away = dot(order[...], far[plane], NT).astype(bf16)
        for at in blocks:
            both = dot(near, g_own[at * rows : (at + 1) * rows, :])
            both += dot(away, g_far[at * rows : (at + 1) * rows, :])
            keep_ref[:, at * span : (at + 1) * span] = both[:half].astype(bf16)
            send_ref[:, at * span : (at + 1) * span] = both[half:].astype(bf16)
    sums = g_own[4 * rows : 4 * rows + 16, :].astype(f32)
    sums += g_far[4 * rows : 4 * rows + 16, :].astype(f32)
    both = dot(order[:, :span], sums[0:8].astype(bf16), NT)
    both += dot(order[:, span:], sums[8:16].astype(bf16), NT)
    tail = jnp.concatenate([both, jnp.zeros((2 * half, LANES - 8), f32)], axis=1).astype(bf16)
    keep_ref[:, 4 * span :] = tail[:half]
    send_ref[:, 4 * span :] = tail[half:]


def attention_grad(order, own, far, g_own, g_far):
    shape = shaped((order.shape[0] // 2, 4 * g_own.shape[1] + LANES), bf16)
    return call(
        attention_grad_kernel,
        "attention_grad",
        [shape, shape],
        flops=2_500_000_000,
    )(order, own, far, g_own, g_far)


def back_kernel(
    side, part_own, part_far, grad_rows, middle, token_rows, gain_one, gain_two,
    w_out, w_in, projected, lse, seg_row, seg_col,
    message, gm_ref, gn_ref, gn_send, bias, branch_low, attended_back,
):
    rows, width = middle.shape
    span = rows // 2
    half = width // 2
    start = side[0] * half

    def mine_of(shift, extent=half):
        return pl.ds(pl.multiple_of(shift + start, LANES), extent)

    unit, scale = layer_norm_parts(middle[...])
    grad = part_own[...].astype(f32)
    grad += jnp.concatenate([part_far[span:, :], part_far[:span, :]], axis=0).astype(f32)
    gains_two = jnp.sum(grad * unit, axis=0, keepdims=True)
    grad_middle = grad_rows[:rows, :].astype(f32) + layer_norm_back(
        grad, gain_two[...], unit, scale
    )
    gm_ref[...] = grad_middle[:span]
    branch_low[...] = grad_middle.astype(bf16)
    attended_back[...] = dot(branch_low[...], w_out[mine_of(0), :], NT).astype(bf16)
    allowed = (seg_col[:, 0:1] == 0) | (seg_col[:, 0:1] == seg_row[0:1, :])
    bias[...] = jnp.where(allowed, 0.0, NEGATIVE)
    first = lax.broadcasted_iota(jnp.int32, (rows, LANES), 1) < HEAD_DIM
    on_side = side[0] == 0
    sums = jnp.transpose(lse[...])

    for p in range(half // LANES):
        def columns(shift):
            return pl.ds(pl.multiple_of(shift + start + p * LANES, LANES), LANES)

        queries = projected[:, columns(0)] * jnp.asarray(SCALE, bf16)
        keys, values = projected[:, columns(width)], projected[:, columns(2 * width)]
        grads = attended_back[:, p * LANES : (p + 1) * LANES]
        parts = []
        for head in range(2):
            mine = first if head == 0 else jnp.logical_not(first)
            zero = jnp.zeros_like(queries)
            at = 2 * p + head
            far_at = at + half // HEAD_DIM
            lse_row = jnp.where(on_side, sums[at : at + 1, :], sums[far_at : far_at + 1, :])
            scores = dot(keys, jnp.where(mine, queries, zero), NT) * LOG2_E + bias[...]
            probs = jnp.exp2(scores - lse_row)
            dprobs = dot(values, jnp.where(mine, grads, zero), NT)
            delta = jnp.sum(probs * dprobs, axis=0, keepdims=True)
            dscores = (probs * (dprobs - delta)).astype(bf16)
            parts.append(
                (
                    dot(dscores, keys, TN) * SCALE,
                    dot(dscores, queries),
                    dot(probs.astype(bf16), grads),
                )
            )
        for at in range(3):
            message[at * rows : (at + 1) * rows, p * LANES : (p + 1) * LANES] = jnp.where(
                first, parts[0][at], parts[1][at]
            ).astype(bf16)
    message[3 * rows : 4 * rows, :] = branch_low[:, mine_of(0)]
    grad_normed = dot(message[0:rows, :], w_in[:, mine_of(0)], NT)
    grad_normed += dot(message[rows : 2 * rows, :], w_in[:, mine_of(width)], NT)
    grad_normed += dot(message[2 * rows : 3 * rows, :], w_in[:, mine_of(2 * width)], NT)
    gn_ref[...] = grad_normed[:span]
    gn_send[...] = grad_normed[span:].astype(bf16)
    unit, _ = layer_norm_parts(token_rows[...])
    gains_one = jnp.sum(grad_normed * unit, axis=0, keepdims=True)
    blank = jnp.zeros((6, half), f32)
    message[4 * rows :, :] = jnp.concatenate(
        [
            gains_one[:, :half], gains_two[:, :half], blank,
            gains_one[:, half:], gains_two[:, half:], blank,
        ],
        axis=0,
    ).astype(bf16)


def back(
    side, part_own, part_far, grad_rows, middle, token_rows, gain_one, gain_two,
    w_out, w_in, projected, lse, seg_row, seg_col,
):
    rows, width = middle.shape
    half, span = width // 2, rows // 2
    return call(
        back_kernel,
        "back",
        [
            shaped((4 * rows + 16, half), bf16),
            shaped((span, width), f32),
            shaped((span, width), f32),
            shaped((span, width), bf16),
        ],
        scratch=[
            pltpu.VMEM((rows, rows), f32),
            pltpu.VMEM((rows, width), bf16),
            pltpu.VMEM((rows, half), bf16),
        ],
        flops=7_000_000_000,
        small=1,
        room=8,
    )(
        side, part_own, part_far, grad_rows, middle, token_rows, gain_one, gain_two,
        w_out, w_in, projected, lse, seg_row, seg_col,
    )


def last_kernel(gm, gn, gn_far, token_rows, gain, out_ref):
    count, span = out_ref.shape[0], gm.shape[0]
    unit, scale = layer_norm_parts(token_rows[...])
    grad = gn[...] + gn_far[...].astype(f32)
    total = gm[...] + layer_norm_back(grad, gain[...], unit, scale)
    out_ref[...] = total[:count].astype(bf16)


def last(gm, gn, gn_far, token_rows, gain, count):
    return call(last_kernel, "last", shaped((count, gm.shape[1]), bf16), flops=10_000_000)(
        gm, gn, gn_far, token_rows, gain
    )


def add_kernel(keep, far, keep_ref, send_ref):
    half = keep_ref.shape[0]
    total = keep[...].astype(f32) + far[...].astype(f32)
    keep_ref[...] = total[:half].astype(bf16)
    send_ref[...] = total[half:].astype(bf16)


def added(keep, far):
    count, wide = keep.shape
    shape = shaped((count // 2, wide), bf16)
    return call(add_kernel, "added", [shape, shape], flops=count * wide)(keep, far)


def finish_kernel(*refs):
    out_ref = refs[-1]
    for e in range(EXPERTS):
        out_ref[e] = refs[2 * e][...].astype(f32) + refs[2 * e + 1][...].astype(f32)


def finished(pairs):
    return call(
        finish_kernel,
        "finished",
        shaped((EXPERTS,) + pairs[0][0].shape, f32),
        flops=pairs[0][0].size * EXPERTS,
    )(*[part for pair in pairs for part in pair])


def body(
    tokens,
    segment_ids,
    expert_ids,
    norm_first,
    project_in,
    project_out,
    norm_second,
    up_weight,
    down_weight,
    cotangent,
):
    own_count, width = tokens.shape[1], tokens.shape[2]
    side = lax.axis_index("blk").astype(jnp.int32)[None]
    count = lax.axis_size("dp")
    place = (lax.axis_index("dp") % INNER).astype(jnp.int32)[None]
    outer = count // INNER
    deep = width // count
    half = width // 2
    gain_one, gain_two = norm_first[None], norm_second[None]

    own_tokens, own_grads = tokens[0], cotangent[0]
    far_tokens = across_blk(own_tokens)
    far_grads = across_blk(own_grads)
    seg_col, seg_row, hot, hot_row, order, half_done, own_normed, own_rows = begin(
        place, side, segment_ids, expert_ids, own_tokens, gain_one, project_in, deep, outer
    )
    rows = hot.shape[0]
    span = rows // 2
    projected, packed, middle, token_rows, lse = front(
        own_rows, own_normed, far_tokens, seg_col, seg_row, gain_one, gain_two,
        project_in, project_out, half_done,
    )
    active, slope, grad_rows = up_forward(packed, hot, hot_row, own_grads, far_grads, up_weight)
    active_far = across_dp(active, CORE)
    grad_rows_far = across_dp(grad_rows, CORE)
    hot_far = grad_rows_far[rows:]
    grad_upward = grad_upward_of(grad_rows, hot, down_weight, slope)
    grad_upward_far = across_dp(grad_upward, CORE)
    packed_far = across_dp(after(packed, grad_upward), CORE)

    cot_own, cot_far = picked(order, hot_row, hot_far, after(grad_rows, grad_upward), grad_rows_far)
    down_raw = [expert_grad(e, cot_own, cot_far, active, active_far) for e in range(EXPERTS)]
    part_own = hidden_back(NT, "grad_normed", after(grad_upward, down_raw), hot, up_weight)
    part_far = across_blk(part_own)
    two_own, two_far = picked(order, hot_row, hot_far, after(packed, part_own), packed_far)
    up_raw = [
        expert_grad(e, two_own, two_far, grad_upward, grad_upward_far) for e in range(EXPERTS)
    ]
    branch = hidden_back(NN, "branch", after(active, up_raw), hot, down_weight)
    branch_far = across_blk(branch[span:])
    layer_out = (
        middle[:own_count] + branch[:own_count].astype(f32) + branch_far[:own_count].astype(f32)
    ).astype(bf16)

    message, gm_own, gn_own, gn_send = back(
        side, after(part_own, branch), part_far, grad_rows, middle, token_rows,
        gain_one, gain_two, project_out, project_in, projected, lse, seg_row, seg_col,
    )
    message_far = across_dp(message, CORE)
    gn_far = across_blk(gn_send)
    in_raw = attention_grad(order, packed, packed_far, message, message_far)
    input_grad = last(gm_own, gn_own, gn_far, own_rows, gain_one, own_count)

    def reduced(keep, send):
        for bit in (NEAR, MID):
            keep, send = added(keep, across_dp(send, bit))
        return keep, across_dp(send, FAR)

    down_sum = finished([reduced(*raw) for raw in down_raw])
    up_sum = finished([reduced(*raw) for raw in up_raw])
    keep, far = reduced(*in_raw)
    in_sum = keep.astype(f32) + far.astype(f32)

    def over_outer(value, axis):
        if outer == 1:
            return value
        groups = [[o * INNER + i for o in range(outer)] for i in range(INNER)]
        return lax.psum_scatter(
            value, "dp", scatter_dimension=axis, tiled=True, axis_index_groups=groups
        )

    up_out = over_outer(up_sum, 1)
    down_out = over_outer(down_sum, 1).transpose(0, 2, 1)
    in_sum = over_outer(in_sum, 0)
    in_far = across_blk(in_sum.astype(bf16)).astype(f32)
    mine = in_sum[:, : 4 * half].reshape(deep, 4, half)
    theirs = in_far[:, : 4 * half].reshape(deep, 4, half)
    joined = jnp.where(
        side[0] == 0,
        jnp.stack([mine, theirs], axis=2),
        jnp.stack([theirs, mine], axis=2),
    ).reshape(deep, 4 * width)
    return (
        layer_out[None],
        input_grad[None],
        in_sum[:, 4 * half] + in_far[:, 4 * half],
        joined[:, : 3 * width],
        joined[:, 3 * width :],
        in_sum[:, 4 * half + 1],
        up_out,
        down_out,
    )


def solution(mesh):
    return jax.shard_map(
        body,
        mesh=mesh,
        in_specs=(
            P("dp", "blk", None),
            P("dp", None),
            P("dp", None),
            P(),
            P(),
            P(),
            P(),
            P(None, None, "blk"),
            P(None, "blk", None),
            P("dp", "blk", None),
        ),
        out_specs=(
            P("dp", "blk", None),
            P("dp", "blk", None),
            P("dp"),
            P("dp", None),
            P("dp", None),
            P("dp"),
            P(None, "dp", "blk"),
            P(None, "blk", "dp"),
        ),
        check_vma=False,
    )
```

```python
import functools

import jax
import jax.numpy as jnp
import numpy as np
from jax import lax
from jax.experimental import pallas as pl
from jax.experimental.pallas import tpu as pltpu
from jax.sharding import PartitionSpec as P

HEAD_DIM = 64
EXPERTS = 3
EPSILON = 1e-05
NEGATIVE = -1e30
ROOT_HALF = 0.7071067811865476
INV_ROOT_TAU = 0.3989422804014327
SCALE = HEAD_DIM ** (-0.5)
LOG2_E = 1.4426950408889634
LANES = 128
CHUNK = 512
UNIT = 256
INNER = 16
CORE, NEAR, MID, FAR = 1, 2, 4, 8
COSTS = {}
HELD_BACK = {None: 1, 'active': 2, 'gu': 8, 'normed': 13, 'cot': 14, 'd0': 15, 'd1': 19, 'two': 20, 'pick': 21, 'u0': 23, 'back': 25, '+d1': 25, '+d0': 25, 'in': 26, 'branch': 29, '+u0': 29, '=d0': 29, '+in': 29, 'u2': 31, 'last': 32, 'u1': 34, '=u0': 34, '+u2': 34, '=in': 34, 'u3': 37, 'down': 37, '+u1': 37, '=u2': 37, '+u3': 37, '=u1': 37, 'sum': 37, '=u3': 37, 'join': 37, 'up': 37}

PIECES = {
    "d0": ((0, 4), (NEAR, MID)),
    "d1": ((4, 6), (MID, NEAR)),
    "u0": ((0, 2), (MID, NEAR)),
    "u1": ((2, 4), (NEAR, MID)),
    "u2": ((4, 5), (NEAR, MID)),
    "u3": ((5, 6), (NEAR, MID)),
    "in": (None, (NEAR, MID)),
}
GROUPS = (("d0", "d1"), ("u0",), ("u1",), ("u2",), ("u3",), ("in",))
STEPS = (
    "gu", "normed", "cot", "d0", "d1", "two", "pick", "u0", "back", "+d1", "+d0", "in", "branch", "+u0", "=d0",
    "+in", "u2", "last", "u1", "=u0", "+u2", "=in", "u3", "down", "+u1", "=u2", "+u3", "=u1", "sum", "=u3",
    "join", "up",
)

f32 = jnp.float32
bf16 = jnp.bfloat16

NN = ((1,), (0,))
NT = ((1,), (1,))


def across_blk(value):
    return lax.ppermute(value, "blk", [(0, 1), (1, 0)])


def across_dp(value, bit):
    count = lax.axis_size("dp")
    return lax.ppermute(value, "dp", [(source, source ^ bit) for source in range(count)])


def dot(a, b, dims=NN):
    return lax.dot_general(a, b, (dims, ((), ())), preferred_element_type=f32)


def layer_norm_parts(values):
    row_mean = jnp.mean(values, axis=-1, keepdims=True)
    centred = values - row_mean
    row_var = jnp.mean(centred * centred, axis=-1, keepdims=True)
    scale = lax.rsqrt(row_var + EPSILON)
    return centred * scale, scale


def layer_norm_back(grad, gain, unit, scale):
    raised = grad * gain
    return scale * (
        raised
        - jnp.mean(raised, axis=-1, keepdims=True)
        - unit * jnp.mean(raised * unit, axis=-1, keepdims=True)
    )


def shaped(shape, dtype):
    return jax.ShapeDtypeStruct(shape, dtype)


def held(shape, dtype):
    size = np.dtype(dtype).itemsize
    shape = (1,) * (2 - len(shape)) + tuple(shape)
    lead = int(np.prod(shape[:-2])) if len(shape) > 2 else 1
    return lead * -(-shape[-2] // 16) * 16 * -(-shape[-1] // LANES) * LANES * size


class Line:
    def __init__(self):
        self.last, self.step = None, None

    def call(self, kernel, name, outs, scratch=(), small=0, large=0, room=3, leaves=False):
        def run(*operands):
            count, total = len(operands), len(outs)
            need = sum(held(v.shape, v.dtype) for v in scratch if v.memory_space == pltpu.VMEM)
            if leaves:
                need += sum(held(v.shape, v.dtype) for v in outs)
                results = list(outs)
            else:
                results = [pltpu.VMEM(v.shape, v.dtype) for v in outs]
            whole = pl.BlockSpec(memory_space=pltpu.VMEM)
            far = pl.BlockSpec(memory_space=pltpu.HBM)
            specs = [pl.BlockSpec(memory_space=pltpu.SMEM)] * small + [far] * large
            specs += [whole] * (count - small - large)
            places = [None] * small + [pltpu.HBM] * large + [pltpu.VMEM] * (count - small - large)
            operands = tuple(
                v if place is None else pltpu.with_memory_space_constraint(v, place)
                for v, place in zip(operands, places)
            )
            if self.last is not None:
                operands += (pltpu.with_memory_space_constraint(self.last, pltpu.HBM),)
                specs.append(far)
            first = len(operands)

            def body_of(*refs):
                kernel(*refs[:count], *refs[first : first + total], *refs[first + total + 1 :])

            *result, self.last = pl.pallas_call(
                body_of,
                name=name,
                out_shape=[*results, pltpu.HBM((HELD_BACK.get(self.step, HELD_BACK[None]) * 2048, LANES), f32)],
                in_specs=specs,
                out_specs=[whole] * total + [far],
                scratch_shapes=list(scratch),
                compiler_params=pltpu.CompilerParams(vmem_limit_bytes=need + room * 2**20),
                cost_estimate=pl.CostEstimate(
                    flops=COSTS.get(self.step, 10) * 10**9, bytes_accessed=1000, transcendentals=0
                ),
            )(*operands)
            return result

        return run


def masked_rows(target, value, hot):
    span = value.shape[1]
    for e in range(EXPERTS):
        target[:, e * span : (e + 1) * span] = value * hot[:, e : e + 1]


def grad_active_of(target, masked, weight):
    width, hidden = weight.shape[2], weight.shape[1]
    for n in range(0, hidden, CHUNK):
        total = dot(masked[:, :width], weight[0, n : n + CHUNK, :], NT)
        for e in range(1, EXPERTS):
            total += dot(masked[:, e * width : (e + 1) * width], weight[e, n : n + CHUNK, :], NT)
        target(slice(n, n + CHUNK), total)


def begin_kernel(
    deep, outer, place, side, ids_hbm, experts_hbm, tokens_hbm, grads_hbm, one_hbm, two_hbm,
    w_in_hbm, down_hbm, up_hbm, w_out_hbm,
    seg_col, seg_row, hot, hot_row, order, gains, own_rows, own_normed, own_cot, projected,
    grad_active, w_in, down, up, w_out,
    ids, experts, tokens, grads, one, two, masked, sems,
):
    pairs = (
        (ids_hbm, ids), (experts_hbm, experts), (tokens_hbm, tokens), (one_hbm, one),
        (grads_hbm, grads), (two_hbm, two), (w_in_hbm, w_in), (down_hbm, down),
        (up_hbm, up), (w_out_hbm, w_out),
    )
    copies = [pltpu.make_async_copy(a, b, sems.at[at]) for at, (a, b) in enumerate(pairs)]
    for copy in copies:
        copy.start()
    rows, (count, width) = seg_col.shape[0], tokens.shape
    span = rows // 2
    on_side = side[0] == 0
    step = outer * deep
    lane = lax.broadcasted_iota(jnp.int32, (step, width), 1)
    low = lax.broadcasted_iota(jnp.int32, (step, width), 0)
    skip = low
    for late in range(1, outer):
        skip += jnp.where(low >= late * deep, (INNER - 1) * deep, 0)
    for block in range(INNER // 2):
        relative = ((block >> 2) & 1) * NEAR + ((block >> 1) & 1) * MID + (block & 1) * FAR
        base = (place[0] ^ relative) * deep
        order[block * step : (block + 1) * step, :] = (lane - base == skip).astype(f32).astype(bf16)
    for copy in copies[:6]:
        copy.wait()

    def both(values):
        halves = values[0:1, :count], values[0:1, count:]
        pad = jnp.full((1, span - count), -1, jnp.int32)
        first = jnp.where(on_side, halves[0], halves[1])
        second = jnp.where(on_side, halves[1], halves[0])
        return jnp.broadcast_to(jnp.concatenate([first, pad, second, pad], axis=1), (8, rows))

    segments, expert = both(ids), both(experts)
    seg_row[...] = segments
    seg_col[...] = jnp.transpose(segments).astype(jnp.int32)
    hot_row[...] = (lax.broadcasted_iota(jnp.int32, (8, rows), 0) == expert).astype(f32)
    hot[...] = (lax.broadcasted_iota(jnp.int32, (rows, 8), 1) == jnp.transpose(expert)).astype(bf16)
    gains[...] = jnp.zeros_like(gains)
    gains[0:1, :] = one[...].reshape(1, width)
    gains[1:2, :] = two[...].reshape(1, width)
    own_cot[...] = jnp.zeros_like(own_cot)
    own_cot[0:count, :] = grads[...]
    own_rows[...] = jnp.zeros_like(own_rows)
    own_rows[0:count, :] = tokens[...]
    unit, _ = layer_norm_parts(own_rows[...].astype(f32))
    normed = (unit * gains[0:1, :]).astype(bf16)
    own_normed[...] = normed
    copies[6].wait()
    projected[...] = dot(normed, w_in[...]).astype(bf16)
    masked_rows(masked, own_cot[...], hot[:span, :])
    copies[7].wait()

    def store(columns, total):
        grad_active[:, columns] = total

    grad_active_of(store, masked, down)
    for copy in copies[8:]:
        copy.wait()


def begin(line, place, side, ids, experts, tokens, grads, one, two, weights, deep, outer):
    count, width = tokens.shape
    hidden = weights[1].shape[1]
    span = -(-count // LANES) * LANES
    rows = 2 * span
    inside = (ids, experts, tokens, grads, one, two)
    return line.call(
        functools.partial(begin_kernel, deep, outer),
        "begin",
        [
            shaped((rows, 8), jnp.int32),
            shaped((8, rows), jnp.int32),
            shaped((rows, 8), bf16),
            shaped((8, rows), f32),
            shaped((width // 2, width), bf16),
            shaped((8, width), f32),
            shaped((span, width), bf16),
            shaped((span, width), bf16),
            shaped((span, width), bf16),
            shaped((span, 3 * width), bf16),
            shaped((span, hidden), f32),
            *[shaped(w.shape, w.dtype) for w in weights],
        ],
        scratch=[
            *[pltpu.VMEM(v.shape, v.dtype) for v in inside],
            pltpu.VMEM((span, EXPERTS * width), bf16),
            pltpu.SemaphoreType.DMA((10,)),
        ],
        small=2,
        large=10,
    )(place, side, *inside, *weights)


def front_kernel(
    side, far, own_rows, own_normed, own_done, seg_col, seg_row, gains, w_in, w_out,
    mine_ref, packed, middle_ref, low_rows, lse_ref, projected, bias,
):
    count, width = far.shape
    rows = projected.shape[0]
    span, own = rows // 2, width // 2
    low_rows[0:span, :] = own_rows[...]
    low_rows[span:, :] = jnp.zeros((span, width), bf16)
    low_rows[span : span + count, :] = far[...]
    unit, _ = layer_norm_parts(low_rows[span:, :].astype(f32))
    normed = (unit * gains[0:1, :]).astype(bf16)
    packed[1, :span, :] = own_normed[...]
    packed[1, span:, :] = normed
    projected[:span, :] = own_done[...]
    projected[span:, :] = dot(normed, w_in[...]).astype(bf16)
    allowed = (seg_col[:, 0:1] == 0) | (seg_col[:, 0:1] == seg_row[0:1, :])
    bias[...] = jnp.where(allowed, 0.0, NEGATIVE)
    first = lax.broadcasted_iota(jnp.int32, (rows, LANES), 1) < HEAD_DIM
    top = lax.broadcasted_iota(jnp.int32, (LANES, rows), 0) < HEAD_DIM
    lse_ref[...] = jnp.zeros_like(lse_ref)
    for p in range(width // LANES):
        columns = slice(p * LANES, (p + 1) * LANES)
        queries = projected[:, columns] * jnp.asarray(SCALE, bf16)
        keys = projected[:, width + p * LANES : width + (p + 1) * LANES]
        values = jnp.transpose(projected[:, 2 * width + p * LANES : 2 * width + (p + 1) * LANES])
        outs = []
        for head in range(2):
            mine, mine_up = (first, top) if head == 0 else (~first, ~top)
            scores = dot(keys, jnp.where(mine, queries, jnp.zeros_like(queries)), NT)
            scores = scores * LOG2_E + bias[...]
            peak = jnp.max(scores, axis=0, keepdims=True)
            raised = jnp.exp2(scores - peak).astype(bf16)
            summed = dot(jnp.where(mine_up, values, jnp.ones_like(values)), raised)
            at = (1 - head) * HEAD_DIM
            total = summed[at : at + 1, :]
            outs.append(summed * (1.0 / total))
            lse_ref[2 * p + head : 2 * p + head + 1, :] = peak + jnp.log2(total)
        packed[2, :, columns] = jnp.transpose(jnp.where(top, outs[0], outs[1])).astype(bf16)
    for at in range(3):
        start = pl.multiple_of(at * width + side[0] * own, LANES)
        mine_ref[:, at * own : (at + 1) * own] = projected[:, pl.ds(start, own)]
    middle = low_rows[...].astype(f32) + dot(packed[2], w_out[...])
    middle_ref[...] = middle
    unit, _ = layer_norm_parts(middle)
    packed[0] = (unit * gains[1:2, :]).astype(bf16)


def front(line, side, far, own_rows, own_normed, own_done, seg_col, seg_row, gains, w_in, w_out):
    span, width = own_rows.shape
    rows = 2 * span
    return line.call(
        front_kernel,
        "front",
        [
            shaped((rows, 3 * width // 2), bf16),
            shaped((3, rows, width), bf16),
            shaped((rows, width), f32),
            shaped((rows, width), bf16),
            shaped((16, rows), f32),
        ],
        scratch=[pltpu.VMEM((rows, 3 * width), bf16), pltpu.VMEM((rows, rows), f32)],
        small=1,
        room=5,
    )(side, far, own_rows, own_normed, own_done, seg_col, seg_row, gains, w_in, w_out)


def plane(message, at, side):
    span = 2 * LANES
    width = message.shape[1] // 2
    start = (2 + at) * span
    return message.at[start : start + span, side * width : (side + 1) * width]


def up_kernel(packed, hot, hot_row, own_cot, far_cot, weight, message, slope_ref, masked):
    _, rows, width = packed.shape
    span, hidden = rows // 2, weight.shape[2]
    masked_rows(masked, packed[0], hot)
    message[:span, hidden:] = own_cot[...]
    message[span:rows, hidden:] = far_cot[...]
    message[rows:, :] = jnp.zeros_like(message[rows:, :])
    message[rows : rows + 8, :rows] = hot_row[...].astype(bf16)
    for n in range(0, hidden, CHUNK):
        part = weight[:, :, n : n + CHUNK].reshape(EXPERTS * width, CHUNK)
        upward = dot(masked[...], part)
        half = 0.5 * (1.0 + lax.erf(upward * ROOT_HALF))
        message[:rows, n : n + CHUNK] = (upward * half).astype(bf16)
        slope_ref[:, n : n + CHUNK] = half + upward * INV_ROOT_TAU * jnp.exp(-0.5 * upward * upward)


def up_forward(line, packed, hot, hot_row, own_cot, far_cot, weight):
    _, rows, width = packed.shape
    hidden = weight.shape[2]
    return line.call(
        up_kernel,
        "up_forward",
        [shaped((rows + 16, hidden + width), bf16), shaped((rows, hidden), f32)],
        scratch=[pltpu.VMEM((rows, EXPERTS * width), bf16)],
        room=5,
    )(packed, hot, hot_row, own_cot, far_cot, weight)


def grad_upward_kernel(far_cot, packed, hot, weight, slope, own_active, out_ref, masked):
    rows = hot.shape[0]
    span = rows // 2
    masked_rows(masked, far_cot[...], hot[span:, :])
    for half in range(2):
        for at in range(3):
            plane(out_ref, at, half)[...] = packed[at, half * span : (half + 1) * span, :]

    def store(columns, total):
        out_ref[:span, columns] = (own_active[:, columns] * slope[:span, columns]).astype(bf16)
        out_ref[span:rows, columns] = (total * slope[span:, columns]).astype(bf16)

    grad_active_of(store, masked, weight)


def grad_upward_of(line, far_cot, packed, hot, weight, slope, own_active):
    _, rows, width = packed.shape
    hidden = weight.shape[1]
    return line.call(
        grad_upward_kernel,
        "grad_upward",
        [shaped((5 * rows // 2, hidden), bf16)],
        scratch=[pltpu.VMEM((rows // 2, EXPERTS * width), bf16)],
        room=5,
    )(far_cot, packed, hot, weight, slope, own_active)


def shortened(rows, count):
    return min(rows // 2, -(-count // 16) * 16)


def normed_kernel(message, hot, weight, out_ref, masked):
    rows, hidden = hot.shape[0], weight.shape[2]
    size = out_ref.shape[0] // 2
    masked_rows(masked, message[:rows, :], hot)
    wide = 256
    for n in range(0, out_ref.shape[1], wide):
        total = dot(masked[:, :hidden], weight[0, n : n + wide, :], NT)
        for e in range(1, EXPERTS):
            total += dot(masked[:, e * hidden : (e + 1) * hidden], weight[e, n : n + wide, :], NT)
        out_ref[:size, n : n + wide] = total[:size].astype(bf16)
        out_ref[size:, n : n + wide] = total[rows // 2 : rows // 2 + size].astype(bf16)


def normed_of(line, message, hot, weight, size):
    rows, hidden = hot.shape[0], weight.shape[2]
    return line.call(
        normed_kernel,
        "grad_normed",
        [shaped((2 * size, weight.shape[1]), bf16)],
        scratch=[pltpu.VMEM((rows, EXPERTS * hidden), bf16)],
        room=5,
    )(message, hot, weight)


def branch_kernel(weight_hbm, sent, hot, own_ref, send_ref, masked, weight, total, sems):
    rows, hidden = hot.shape[0], weight.shape[1]
    size, width = own_ref.shape
    copies = []
    for e in range(EXPERTS):
        copies.append(pltpu.make_async_copy(weight_hbm.at[e], weight.at[e], sems.at[e]))
        copies[-1].start()
    masked_rows(masked, sent[:rows, :hidden], hot)
    for e in range(EXPERTS):
        copies[e].wait()
        part = masked[:, e * hidden : (e + 1) * hidden]
        for n in range(0, width, 256):
            columns = slice(n, n + 256)
            done = dot(part, weight[e, :, columns])
            if e > 0:
                done += total[:, columns]
            if e < EXPERTS - 1:
                total[:, columns] = done
            else:
                own_ref[:, columns] = done[:size].astype(bf16)
                send_ref[:, columns] = done[rows // 2 : rows // 2 + size].astype(bf16)


def branch_of(line, weight, sent, hot, size):
    rows, (_, hidden, width) = hot.shape[0], weight.shape
    shape = shaped((size, width), bf16)
    return line.call(
        branch_kernel,
        "branch",
        [shape, shape],
        scratch=[
            pltpu.VMEM((rows, EXPERTS * hidden), bf16),
            pltpu.VMEM(weight.shape, weight.dtype),
            pltpu.VMEM((rows, width), f32),
            pltpu.SemaphoreType.DMA((EXPERTS,)),
        ],
        large=1,
        room=5,
    )(weight, sent, hot)


def masked_turned(order, rows, hot, target, part):
    turned = dot(order[...], rows, NT)
    for e in range(EXPERTS):
        target[e, :, part] = (turned * hot[e : e + 1, part].astype(f32)).astype(bf16)


def picked_grads_kernel(order, hot_own, own, far, own_ref, far_ref):
    rows, width = own_ref.shape[2], order.shape[1]
    hidden = own.shape[1] - width
    every = slice(0, rows)
    masked_turned(order, own[:rows, hidden:], hot_own, own_ref, every)
    masked_turned(order, far[:rows, hidden:], far.at[rows:, :], far_ref, every)


def picked_grads(line, order, hot_own, own, far):
    shape = shaped((EXPERTS, order.shape[0], hot_own.shape[1]), bf16)
    return line.call(picked_grads_kernel, "picked", [shape, shape])(order, hot_own, own, far)


def picked_kernel(order, hot_own, first, own, far, own_ref, far_ref):
    rows = own_ref.shape[2]
    span = rows // 2
    for source, hot, target in ((own, hot_own, own_ref), (far, first.at[rows:, :], far_ref)):
        for half in range(2):
            part = slice(half * span, (half + 1) * span)
            masked_turned(order, plane(source, 0, half)[...], hot, target, part)


def picked(line, order, hot_own, first, own, far):
    shape = shaped((EXPERTS, order.shape[0], hot_own.shape[1]), bf16)
    return line.call(picked_kernel, "picked", [shape, shape])(order, hot_own, first, own, far)


def turned_kernel(order, own, far, out_ref):
    span = out_ref.shape[2] // 2
    for at, (source, part) in enumerate(((own, 1), (far, 1), (own, 2), (far, 2))):
        for half in range(2):
            turned = dot(order[...], plane(source, part, half)[...], NT)
            out_ref[at, :, half * span : (half + 1) * span] = turned.astype(bf16)


def turned(line, order, own, far, rows):
    shape = shaped((4, order.shape[0], rows), bf16)
    return line.call(turned_kernel, "turned", [shape])(order, own, far)


def split_store(first, value, columns, keep_ref, send_ref):
    value = value.astype(bf16)
    half, quarter = value.shape[0] // 2, value.shape[0] // 4
    if first == NEAR:
        keep_ref[:, columns] = value[:half]
        send_ref[:, columns] = value[half:]
    else:
        for part in range(2):
            rows = slice(part * quarter, (part + 1) * quarter)
            keep_ref[rows, columns] = value[part * half : part * half + quarter]
            send_ref[rows, columns] = value[part * half + quarter : (part + 1) * half]


def expert_grad_kernel(first, start, stop, a_own, a_far, own, far, keep_ref, send_ref):
    rows = a_own.shape[2]
    for n in range(start, stop, CHUNK):
        wide = min(CHUNK, stop - n)
        for e in range(EXPERTS):
            both = dot(a_own[e], own[:rows, n : n + wide]) + dot(a_far[e], far[:rows, n : n + wide])
            at = e * (stop - start) + n - start
            split_store(first, both, slice(at, at + wide), keep_ref, send_ref)


def expert_grad(line, first, sides, own, far, start, stop):
    shape = shaped((sides[0].shape[1] // 2, EXPERTS * (stop - start)), bf16)
    return line.call(
        functools.partial(expert_grad_kernel, first, start, stop),
        "expert_grad",
        [shape, shape],
        room=4,
    )(*sides, own, far)


def attention_grad_kernel(first, order, sides, g_own, g_far, keep_ref, send_ref):
    rows, span = sides.shape[2], g_own.shape[1]
    for at in range(4):
        part = slice(at * rows, (at + 1) * rows)
        pair = 0 if at < 3 else 2
        both = dot(sides[pair], g_own[part, :]) + dot(sides[pair + 1], g_far[part, :])
        split_store(first, both, slice(at * span, (at + 1) * span), keep_ref, send_ref)
    sums = g_own[4 * rows : 4 * rows + 16, :].astype(f32)
    sums += g_far[4 * rows : 4 * rows + 16, :].astype(f32)
    both = dot(order[:, :span], sums[0:8].astype(bf16), NT)
    both += dot(order[:, span:], sums[8:16].astype(bf16), NT)
    tail = jnp.concatenate([both, jnp.zeros((both.shape[0], LANES - 8), f32)], axis=1)
    split_store(first, tail, slice(4 * span, 4 * span + LANES), keep_ref, send_ref)


def attention_grad(line, first, order, sides, g_own, g_far):
    shape = shaped((order.shape[0] // 2, 4 * g_own.shape[1] + LANES), bf16)
    return line.call(
        functools.partial(attention_grad_kernel, first), "attention_grad", [shape, shape]
    )(order, sides, g_own, g_far)


def back_kernel(
    side, w_in_hbm, w_out_hbm, part_own, part_far, own_cot, far_cot, middle, low_rows, gains, mine_ref,
    lse, seg_row, seg_col,
    message, gm_ref, gn_ref, gn_send, bias, branch_low, attended_back, w_in, w_out, sems,
):
    rows, width = middle.shape
    span, own = rows // 2, width // 2
    size = gn_send.shape[0]
    start = side[0] * own
    copies = [pltpu.make_async_copy(w_out_hbm.at[pl.ds(start, own), :], w_out, sems.at[3])]
    for at in range(3):
        columns = pl.ds(pl.multiple_of(at * width + start, LANES), own)
        copies.append(pltpu.make_async_copy(w_in_hbm.at[:, columns], w_in.at[at], sems.at[at]))
    for copy in copies:
        copy.start()
    unit, scale = layer_norm_parts(middle[...])
    blank = jnp.zeros((span - size, width), f32)
    first = part_own[:size, :].astype(f32) + part_far[size:, :].astype(f32)
    second = part_own[size:, :].astype(f32) + part_far[:size, :].astype(f32)
    grad = jnp.concatenate([first, blank, second, blank], axis=0)
    gains_two = jnp.sum(grad * unit, axis=0, keepdims=True)
    grads_low = jnp.concatenate([own_cot[...], far_cot[...]], axis=0)
    grad_middle = grads_low.astype(f32) + layer_norm_back(grad, gains[1:2, :], unit, scale)
    gm_ref[...] = grad_middle[:span]
    branch_low[...] = grad_middle.astype(bf16)
    copies[0].wait()
    attended_back[...] = dot(branch_low[...], w_out[...], NT).astype(bf16)
    allowed = (seg_col[:, 0:1] == 0) | (seg_col[:, 0:1] == seg_row[0:1, :])
    bias[...] = jnp.where(allowed, 0.0, NEGATIVE)
    first = lax.broadcasted_iota(jnp.int32, (rows, LANES), 1) < HEAD_DIM
    top = lax.broadcasted_iota(jnp.int32, (LANES, rows), 0) < HEAD_DIM
    on_side = side[0] == 0
    for p in range(own // LANES):
        columns = slice(p * LANES, (p + 1) * LANES)
        queries = mine_ref[:, columns] * jnp.asarray(SCALE, bf16)
        keys = mine_ref[:, own + p * LANES : own + (p + 1) * LANES]
        values = mine_ref[:, 2 * own + p * LANES : 2 * own + (p + 1) * LANES]
        grads = attended_back[:, columns]
        keys_up = jnp.transpose(keys)
        parts = []
        for head in range(2):
            mine = first if head == 0 else jnp.logical_not(first)
            zero = jnp.zeros_like(queries)
            at = 2 * p + head
            far_at = at + own // HEAD_DIM
            lse_row = jnp.where(on_side, lse[at : at + 1, :], lse[far_at : far_at + 1, :])
            scores = dot(keys, jnp.where(mine, queries, zero), NT) * LOG2_E + bias[...]
            probs = jnp.exp2(scores - lse_row)
            dprobs = dot(values, jnp.where(mine, grads, zero), NT)
            delta = jnp.sum(probs * dprobs, axis=0, keepdims=True)
            dscores = (probs * (dprobs - delta)).astype(bf16)
            parts.append(
                (
                    dot(keys_up, dscores) * SCALE,
                    dot(dscores, queries),
                    dot(probs.astype(bf16), grads),
                )
            )
        turned_back = jnp.where(top, parts[0][0], parts[1][0])
        message[0:rows, columns] = jnp.transpose(turned_back).astype(bf16)
        for at in range(1, 3):
            message[at * rows : (at + 1) * rows, columns] = jnp.where(
                first, parts[0][at], parts[1][at]
            ).astype(bf16)
    message[3 * rows : 4 * rows, :] = branch_low[:, pl.ds(pl.multiple_of(start, LANES), own)]
    for copy in copies[1:]:
        copy.wait()
    grad_normed = dot(message[0:rows, :], w_in[0], NT)
    grad_normed += dot(message[rows : 2 * rows, :], w_in[1], NT)
    grad_normed += dot(message[2 * rows : 3 * rows, :], w_in[2], NT)
    gn_ref[...] = grad_normed[:span]
    gn_send[...] = grad_normed[span : span + size].astype(bf16)
    unit, _ = layer_norm_parts(low_rows[...].astype(f32))
    gains_one = jnp.sum(grad_normed * unit, axis=0, keepdims=True)
    blank = jnp.zeros((6, own), f32)
    message[4 * rows :, :] = jnp.concatenate(
        [
            gains_one[:, :own], gains_two[:, :own], blank,
            gains_one[:, own:], gains_two[:, own:], blank,
        ],
        axis=0,
    ).astype(bf16)


def back(
    line, side, w_in, w_out, part_own, part_far, own_cot, far_cot, middle, low_rows, gains, mine, lse,
    seg_row, seg_col,
):
    rows, width = middle.shape
    own, span, size = width // 2, rows // 2, part_own.shape[0] // 2
    return line.call(
        back_kernel,
        "back",
        [
            shaped((4 * rows + 16, own), bf16),
            shaped((span, width), f32),
            shaped((span, width), f32),
            shaped((size, width), bf16),
        ],
        scratch=[
            pltpu.VMEM((rows, rows), f32),
            pltpu.VMEM((rows, width), bf16),
            pltpu.VMEM((rows, own), bf16),
            pltpu.VMEM((3, width, own), bf16),
            pltpu.VMEM((own, width), bf16),
            pltpu.SemaphoreType.DMA((4,)),
        ],
        small=1,
        large=2,
        room=7,
    )(
        side, w_in, w_out, part_own, part_far, own_cot, far_cot, middle, low_rows, gains, mine, lse,
        seg_row, seg_col,
    )


def last_kernel(gm, gn, gn_far, low_rows, gains, middle, branch, branch_far, out_ref, layer_ref):
    count, size = out_ref.shape[0], gn_far.shape[0]
    unit, scale = layer_norm_parts(low_rows[:size, :].astype(f32))
    grad = gn[:size, :] + gn_far[...].astype(f32)
    total = gm[:size, :] + layer_norm_back(grad, gains[0:1, :], unit, scale)
    out_ref[...] = total[:count].astype(bf16)
    total = middle[:size, :] + branch[...].astype(f32) + branch_far[...].astype(f32)
    layer_ref[...] = total[:count].astype(bf16)


def last(line, gm, gn, gn_far, low_rows, gains, middle, branch, branch_far, count):
    shape = shaped((count, gm.shape[1]), bf16)
    return line.call(last_kernel, "last", [shape, shape], leaves=True)(
        gm, gn, gn_far, low_rows, gains, middle, branch, branch_far
    )


def add_kernel(*refs):
    keep_ref, send_ref = refs[-2:]
    half, at = keep_ref.shape[0], 0
    for keep, far in zip(refs[0:-2:2], refs[1:-2:2]):
        columns = slice(at, at + keep.shape[1])
        total = keep[...].astype(f32) + far[...].astype(f32)
        keep_ref[:, columns] = total[:half].astype(bf16)
        send_ref[:, columns] = total[half:].astype(bf16)
        at += keep.shape[1]


def added(line, pairs):
    count, wide = pairs[0][0].shape[0], sum(pair[0].shape[1] for pair in pairs)
    shape = shaped((count // 2, wide), bf16)
    return line.call(add_kernel, "added", [shape, shape])(*[v for pair in pairs for v in pair])


def finish_kernel(places, *refs):
    out_ref, start = refs[-1], 0
    for (pair, at, wide) in places:
        keep, far = refs[2 * pair], refs[2 * pair + 1]
        for e in range(EXPERTS):
            columns = slice(at + e * wide, at + (e + 1) * wide)
            out_ref[e, :, start : start + wide] = keep[:, columns].astype(f32) + far[:, columns].astype(f32)
        start += wide


def finished(line, pairs, places):
    shape = (EXPERTS, pairs[0][0].shape[0], sum(place[2] for place in places))
    kernel = functools.partial(finish_kernel, places)
    return line.call(kernel, "finished", [shaped(shape, f32)], leaves=True)(
        *[v for pair in pairs for v in pair]
    )[0]


def summed_kernel(at, keep, far, out_ref, low_ref):
    columns = slice(at, at + out_ref.shape[1])
    total = keep[:, columns].astype(f32) + far[:, columns].astype(f32)
    out_ref[...] = total
    low_ref[...] = total.astype(bf16)


def summed(line, keep, far, at, wide):
    shape = (keep.shape[0], wide)
    return line.call(
        functools.partial(summed_kernel, at), "summed", [shaped(shape, f32), shaped(shape, bf16)]
    )(keep, far)


def joined_kernel(side, own, far, in_ref, out_ref, gain_ref):
    half = out_ref.shape[1] // 2
    on_side = side[0] == 0
    for at in range(4):
        columns = slice(at * half, (at + 1) * half)
        mine, theirs = own[:, columns], far[:, columns].astype(f32)
        target, start = (in_ref, 2 * at * half) if at < 3 else (out_ref, 0)
        target[:, start : start + half] = jnp.where(on_side, mine, theirs)
        target[:, start + half : start + 2 * half] = jnp.where(on_side, theirs, mine)
    both = own[:, 4 * half :] + far[:, 4 * half :].astype(f32)
    kind = lax.broadcasted_iota(jnp.int32, both.shape, 1)
    gain_ref[...] = jnp.where(kind == 0, both, own[:, 4 * half :])


def joined(line, side, own, far):
    count, wide = own.shape
    half = (wide - LANES) // 4
    return line.call(
        joined_kernel,
        "joined",
        [shaped((count, 6 * half), f32), shaped((count, 2 * half), f32), shaped((count, LANES), f32)],
        small=1,
        leaves=True,
    )(side, own, far)


def body(
    tokens,
    segment_ids,
    expert_ids,
    norm_first,
    project_in,
    project_out,
    norm_second,
    up_weight,
    down_weight,
    cotangent,
):
    own_count, width = tokens.shape[1], tokens.shape[2]
    side = lax.axis_index("blk").astype(jnp.int32)[None]
    count = lax.axis_size("dp")
    place = (lax.axis_index("dp") % INNER).astype(jnp.int32)[None]
    outer = count // INNER
    deep = width // count
    line = Line()

    own_tokens, own_grads = tokens[0], cotangent[0]
    far_tokens = across_blk(own_tokens)
    (
        seg_col, seg_row, hot, hot_row, order, gains, own_rows, own_normed, own_cot, own_done,
        own_active, w_in, w_down, w_up, w_out,
    ) = begin(
        line, place, side, segment_ids, expert_ids, own_tokens, own_grads, norm_first, norm_second,
        (project_in, down_weight, up_weight, project_out), deep, outer,
    )
    far_cot = across_blk(own_cot)
    rows = hot.shape[0]
    size = shortened(rows, own_count)
    mine, packed, middle, low_rows, lse = front(
        line, side, far_tokens, own_rows, own_normed, own_done, seg_col, seg_row, gains, w_in, w_out
    )
    line.step = "active"
    sent, slope = up_forward(line, packed, hot, hot_row, own_cot, far_cot, w_up)
    sent_far = across_dp(sent, CORE)

    def over_outer(value, axis):
        if outer == 1:
            return value
        groups = [[o * INNER + i for o in range(outer)] for i in range(INNER)]
        return lax.psum_scatter(
            value, "dp", scatter_dimension=axis, tiled=True, axis_index_groups=groups
        )

    state, made, places = {}, {}, {}

    def send(name, axis, keep, going):
        state[name] = (keep, across_dp(going, axis))

    for step in STEPS:
        line.step = step
        if step[0] == "+":
            send(step[1:], PIECES[step[1:]][1][1], *added(line, [state[step[1:]]]))
        elif step[0] == "=":
            (group,) = [names for names in GROUPS if names[0] == step[1:]]
            at = 0
            for name in group:
                places[name] = (step, at)
                at += state[name][0].shape[1]
            send(step, FAR, *added(line, [state[name] for name in group]))
        elif step == "in":
            axis = PIECES[step][1][0]
            send(step, axis, *attention_grad(line, axis, order, sides, message, message_far))
        elif step in PIECES:
            (start, stop), (axis, _) = PIECES[step]
            pair = (later, later_far) if step[0] == "u" else (sent, sent_far)
            send(step, axis, *expert_grad(line, axis, made[step[0]], *pair, start * UNIT, stop * UNIT))
        elif step == "gu":
            (later,) = grad_upward_of(line, far_cot, packed, hot, w_down, slope, own_active)
            later_far = across_dp(later, CORE)
        elif step == "normed":
            (part_own,) = normed_of(line, later, hot, w_up, size)
            part_far = across_blk(part_own)
        elif step == "branch":
            branch, branch_send = branch_of(line, down_weight, sent, hot, size)
            branch_far = across_blk(branch_send)
        elif step == "cot":
            made["d"] = picked_grads(line, order, hot_row, sent, sent_far)
        elif step == "two":
            made["u"] = picked(line, order, hot_row, sent_far, later, later_far)
        elif step == "pick":
            (sides,) = turned(line, order, later, later_far, rows)
        elif step == "back":
            message, gm_own, gn_own, gn_send = back(
                line, side, project_in, project_out, part_own, part_far, own_cot, far_cot, middle,
                low_rows, gains, mine, lse, seg_row, seg_col,
            )
            message_far = across_dp(message, CORE)
            gn_far = across_blk(gn_send)
        elif step == "last":
            input_grad, layer_out = last(
                line, gm_own, gn_own, gn_far, low_rows, gains, middle, branch, branch_far, own_count
            )
        elif step in ("down", "up"):
            names = sorted(n for n in PIECES if n[0] == step[0])
            groups = sorted({places[n][0] for n in names})
            cut = [
                (groups.index(places[n][0]), places[n][1], (PIECES[n][0][1] - PIECES[n][0][0]) * UNIT)
                for n in names
            ]
            made[step] = finished(line, [state[g] for g in groups], cut)
        elif step == "sum":
            wide = 2 * width + LANES
            in_sum, in_low = summed(line, *state[places["in"][0]], places["in"][1], wide)
            if outer > 1:
                in_sum = over_outer(in_sum, 0)
                in_low = in_sum.astype(bf16)
            in_far = across_blk(in_low)
        elif step == "join":
            in_out, out_out, gain_out = joined(line, side, in_sum, in_far)

    up_out = over_outer(made["up"], 1)
    down_out = over_outer(made["down"], 1).transpose(0, 2, 1)
    return (
        layer_out[None],
        input_grad[None],
        gain_out[:, 0],
        in_out,
        out_out,
        gain_out[:, 1],
        up_out,
        down_out,
    )


def solution(mesh):
    return jax.shard_map(
        body,
        mesh=mesh,
        in_specs=(
            P("dp", "blk", None),
            P("dp", None),
            P("dp", None),
            P(),
            P(),
            P(),
            P(),
            P(None, None, "blk"),
            P(None, "blk", None),
            P("dp", "blk", None),
        ),
        out_specs=(
            P("dp", "blk", None),
            P("dp", "blk", None),
            P("dp"),
            P("dp", None),
            P("dp", None),
            P("dp"),
            P(None, "dp", "blk"),
            P(None, "blk", "dp"),
        ),
        check_vma=False,
    )
```

```python
import functools

import jax
import jax.numpy as jnp
import numpy as np
from jax import lax
from jax.experimental import pallas as pl
from jax.experimental.pallas import tpu as pltpu
from jax.sharding import PartitionSpec as P

HEAD_DIM = 64
EXPERTS = 3
EPSILON = 1e-05
NEGATIVE = -1e30
ROOT_HALF = 0.7071067811865476
INV_ROOT_TAU = 0.3989422804014327
SCALE = HEAD_DIM ** (-0.5)
LOG2_E = 1.4426950408889634
LANES = 128
CHUNK = 512
UNIT = 256
INNER = 16
CORE, NEAR, MID, FAR = 1, 2, 4, 8
COSTS = {'down': 3}
HELD_BACK = {None: 1, 'active': 2, 'half': 6, 'gu': 12, 'cot': 13, 'd0': 14, 'd1': 18, 'rest': 23, 'two': 24, 'pick': 25, 'u3': 27, 'weights': 28, 'back': 30, '+d1': 30, '+d0': 30, 'in': 31, 'u2': 33, 'branch': 36, '=d0': 36, '+u3': 42, '+in': 42, 'u0': 44, 'last': 45, '+u2': 45, '=in': 45, 'u1': 48, '+u0': 48, '=u2': 48, 'down': 48, '+u1': 48, 'sum': 48, '=u0': 48, 'join': 48, '=u1': 48, 'up': 48}

PIECES = {
    "d0": ((0, 4), (MID, NEAR)),
    "d1": ((4, 6), (NEAR, MID)),
    "u0": ((0, 1), (NEAR, MID)),
    "u1": ((1, 2), (NEAR, MID)),
    "u2": ((2, 4), (NEAR, MID)),
    "u3": ((4, 6), (NEAR, MID)),
    "in": (None, (MID, NEAR)),
}
GROUPS = (("in",), ("d0", "d1"), ("u2", "u3"), ("u0",), ("u1",))
STEPS = (
    "half", "gu", "cot", "d0", "d1", "two", "rest", "pick", "u3", "weights", "back", "+d1", "+d0", "in", "u2",
    "branch", "=d0", "+u3", "+in", "u0", "last", "+u2", "=in", "u1", "+u0", "=u2", "down", "+u1", "sum", "=u0",
    "join", "=u1", "up",
)

f32 = jnp.float32
bf16 = jnp.bfloat16

NN = ((1,), (0,))
NT = ((1,), (1,))


def across_blk(value):
    return lax.ppermute(value, "blk", [(0, 1), (1, 0)])


def across_dp(value, bit):
    count = lax.axis_size("dp")
    return lax.ppermute(value, "dp", [(source, source ^ bit) for source in range(count)])


def dot(a, b, dims=NN):
    return lax.dot_general(a, b, (dims, ((), ())), preferred_element_type=f32)


def layer_norm_parts(values):
    row_mean = jnp.mean(values, axis=-1, keepdims=True)
    centred = values - row_mean
    row_var = jnp.mean(centred * centred, axis=-1, keepdims=True)
    scale = lax.rsqrt(row_var + EPSILON)
    return centred * scale, scale


def layer_norm_back(grad, gain, unit, scale):
    raised = grad * gain
    return scale * (
        raised
        - jnp.mean(raised, axis=-1, keepdims=True)
        - unit * jnp.mean(raised * unit, axis=-1, keepdims=True)
    )


def shaped(shape, dtype):
    return jax.ShapeDtypeStruct(shape, dtype)


def held(shape, dtype):
    size = np.dtype(dtype).itemsize
    shape = (1,) * (2 - len(shape)) + tuple(shape)
    lead = int(np.prod(shape[:-2])) if len(shape) > 2 else 1
    return lead * -(-shape[-2] // 16) * 16 * -(-shape[-1] // LANES) * LANES * size


class Line:
    def __init__(self):
        self.last, self.step = None, None

    def call(self, kernel, name, outs, scratch=(), small=0, large=0, room=3, leaves=False):
        def run(*operands):
            count, total = len(operands), len(outs)
            need = sum(held(v.shape, v.dtype) for v in scratch if v.memory_space == pltpu.VMEM)
            if leaves:
                need += sum(held(v.shape, v.dtype) for v in outs)
                results = list(outs)
            else:
                results = [pltpu.VMEM(v.shape, v.dtype) for v in outs]
            whole = pl.BlockSpec(memory_space=pltpu.VMEM)
            far = pl.BlockSpec(memory_space=pltpu.HBM)
            specs = [pl.BlockSpec(memory_space=pltpu.SMEM)] * small + [far] * large
            specs += [whole] * (count - small - large)
            places = [None] * small + [pltpu.HBM] * large + [pltpu.VMEM] * (count - small - large)
            operands = tuple(
                v if place is None else pltpu.with_memory_space_constraint(v, place)
                for v, place in zip(operands, places)
            )
            if self.last is not None:
                operands += (pltpu.with_memory_space_constraint(self.last, pltpu.HBM),)
                specs.append(far)
            first = len(operands)

            def body_of(*refs):
                kernel(*refs[:count], *refs[first : first + total], *refs[first + total + 1 :])

            *result, self.last = pl.pallas_call(
                body_of,
                name=name,
                out_shape=[*results, pltpu.HBM((HELD_BACK.get(self.step, HELD_BACK[None]) * 2048, LANES), f32)],
                in_specs=specs,
                out_specs=[whole] * total + [far],
                scratch_shapes=list(scratch),
                compiler_params=pltpu.CompilerParams(vmem_limit_bytes=need + room * 2**20),
                cost_estimate=pl.CostEstimate(
                    flops=COSTS.get(self.step, 10) * 10**9, bytes_accessed=1000, transcendentals=0
                ),
            )(*operands)
            return result

        return run


def masked_rows(target, value, hot):
    span = value.shape[1]
    for e in range(EXPERTS):
        target[:, e * span : (e + 1) * span] = value * hot[:, e : e + 1]


def grad_active_of(target, masked, weight):
    width, hidden = weight.shape[2], weight.shape[1]
    for n in range(0, hidden, CHUNK):
        total = dot(masked[:, :width], weight[0, n : n + CHUNK, :], NT)
        for e in range(1, EXPERTS):
            total += dot(masked[:, e * width : (e + 1) * width], weight[e, n : n + CHUNK, :], NT)
        target(slice(n, n + CHUNK), total)


def begin_kernel(
    deep, outer, place, side, ids_hbm, experts_hbm, tokens_hbm, grads_hbm, one_hbm, two_hbm,
    w_in_hbm, down_hbm, up_hbm, w_out_hbm,
    seg_col, seg_row, hot, hot_row, order, gains, own_rows, own_normed, own_cot, projected,
    grad_active, w_in, down, up, w_out,
    ids, experts, tokens, grads, one, two, masked, sems,
):
    pairs = (
        (ids_hbm, ids), (experts_hbm, experts), (tokens_hbm, tokens), (one_hbm, one),
        (grads_hbm, grads), (two_hbm, two), (w_in_hbm, w_in), (down_hbm, down),
        (up_hbm, up), (w_out_hbm, w_out),
    )
    copies = [pltpu.make_async_copy(a, b, sems.at[at]) for at, (a, b) in enumerate(pairs)]
    for copy in copies:
        copy.start()
    rows, (count, width) = seg_col.shape[0], tokens.shape
    span = rows // 2
    on_side = side[0] == 0
    step = outer * deep
    lane = lax.broadcasted_iota(jnp.int32, (step, width), 1)
    low = lax.broadcasted_iota(jnp.int32, (step, width), 0)
    skip = low
    for late in range(1, outer):
        skip += jnp.where(low >= late * deep, (INNER - 1) * deep, 0)
    for block in range(INNER // 2):
        relative = ((block >> 2) & 1) * NEAR + ((block >> 1) & 1) * MID + (block & 1) * FAR
        base = (place[0] ^ relative) * deep
        order[block * step : (block + 1) * step, :] = (lane - base == skip).astype(f32).astype(bf16)
    for copy in copies[:6]:
        copy.wait()

    def both(values):
        halves = values[0:1, :count], values[0:1, count:]
        pad = jnp.full((1, span - count), -1, jnp.int32)
        first = jnp.where(on_side, halves[0], halves[1])
        second = jnp.where(on_side, halves[1], halves[0])
        return jnp.broadcast_to(jnp.concatenate([first, pad, second, pad], axis=1), (8, rows))

    segments, expert = both(ids), both(experts)
    seg_row[...] = segments
    seg_col[...] = jnp.transpose(segments).astype(jnp.int32)
    hot_row[...] = (lax.broadcasted_iota(jnp.int32, (8, rows), 0) == expert).astype(f32)
    hot[...] = (lax.broadcasted_iota(jnp.int32, (rows, 8), 1) == jnp.transpose(expert)).astype(bf16)
    gains[...] = jnp.zeros_like(gains)
    gains[0:1, :] = one[...].reshape(1, width)
    gains[1:2, :] = two[...].reshape(1, width)
    own_cot[...] = jnp.zeros_like(own_cot)
    own_cot[0:count, :] = grads[...]
    own_rows[...] = jnp.zeros_like(own_rows)
    own_rows[0:count, :] = tokens[...]
    unit, _ = layer_norm_parts(own_rows[...].astype(f32))
    normed = (unit * gains[0:1, :]).astype(bf16)
    own_normed[...] = normed
    copies[6].wait()
    projected[...] = dot(normed, w_in[...]).astype(bf16)
    masked_rows(masked, own_cot[...], hot[:span, :])
    copies[7].wait()

    def store(columns, total):
        grad_active[:, columns] = total

    grad_active_of(store, masked, down)
    for copy in copies[8:]:
        copy.wait()


def begin(line, place, side, ids, experts, tokens, grads, one, two, weights, deep, outer):
    count, width = tokens.shape
    hidden = weights[1].shape[1]
    span = -(-count // LANES) * LANES
    rows = 2 * span
    inside = (ids, experts, tokens, grads, one, two)
    return line.call(
        functools.partial(begin_kernel, deep, outer),
        "begin",
        [
            shaped((rows, 8), jnp.int32),
            shaped((8, rows), jnp.int32),
            shaped((rows, 8), bf16),
            shaped((8, rows), f32),
            shaped((width // 2, width), bf16),
            shaped((8, width), f32),
            shaped((span, width), bf16),
            shaped((span, width), bf16),
            shaped((span, width), bf16),
            shaped((span, 3 * width), bf16),
            shaped((span, hidden), f32),
            *[shaped(w.shape, w.dtype) for w in weights],
        ],
        scratch=[
            *[pltpu.VMEM(v.shape, v.dtype) for v in inside],
            pltpu.VMEM((span, EXPERTS * width), bf16),
            pltpu.SemaphoreType.DMA((10,)),
        ],
        small=2,
        large=10,
    )(place, side, *inside, *weights)


def front_kernel(
    side, far, own_rows, own_normed, own_done, seg_col, seg_row, gains, w_in, w_out,
    mine_ref, packed, middle_ref, low_rows, lse_ref, projected, bias,
):
    count, width = far.shape
    rows = projected.shape[0]
    span, own = rows // 2, width // 2
    low_rows[0:span, :] = own_rows[...]
    low_rows[span:, :] = jnp.zeros((span, width), bf16)
    low_rows[span : span + count, :] = far[...]
    unit, _ = layer_norm_parts(low_rows[span:, :].astype(f32))
    normed = (unit * gains[0:1, :]).astype(bf16)
    packed[1, :span, :] = own_normed[...]
    packed[1, span:, :] = normed
    projected[:span, :] = own_done[...]
    projected[span:, :] = dot(normed, w_in[...]).astype(bf16)
    allowed = (seg_col[:, 0:1] == 0) | (seg_col[:, 0:1] == seg_row[0:1, :])
    bias[...] = jnp.where(allowed, 0.0, NEGATIVE)
    first = lax.broadcasted_iota(jnp.int32, (rows, LANES), 1) < HEAD_DIM
    top = lax.broadcasted_iota(jnp.int32, (LANES, rows), 0) < HEAD_DIM
    lse_ref[...] = jnp.zeros_like(lse_ref)
    for p in range(width // LANES):
        columns = slice(p * LANES, (p + 1) * LANES)
        queries = projected[:, columns] * jnp.asarray(SCALE, bf16)
        keys = projected[:, width + p * LANES : width + (p + 1) * LANES]
        values = jnp.transpose(projected[:, 2 * width + p * LANES : 2 * width + (p + 1) * LANES])
        outs = []
        for head in range(2):
            mine, mine_up = (first, top) if head == 0 else (~first, ~top)
            scores = dot(keys, jnp.where(mine, queries, jnp.zeros_like(queries)), NT)
            scores = scores * LOG2_E + bias[...]
            peak = jnp.max(scores, axis=0, keepdims=True)
            raised = jnp.exp2(scores - peak).astype(bf16)
            summed = dot(jnp.where(mine_up, values, jnp.ones_like(values)), raised)
            at = (1 - head) * HEAD_DIM
            total = summed[at : at + 1, :]
            outs.append(summed * (1.0 / total))
            lse_ref[2 * p + head : 2 * p + head + 1, :] = peak + jnp.log2(total)
        packed[2, :, columns] = jnp.transpose(jnp.where(top, outs[0], outs[1])).astype(bf16)
    for at in range(3):
        start = pl.multiple_of(at * width + side[0] * own, LANES)
        mine_ref[:, at * own : (at + 1) * own] = projected[:, pl.ds(start, own)]
    middle = low_rows[...].astype(f32) + dot(packed[2], w_out[...])
    middle_ref[...] = middle
    unit, _ = layer_norm_parts(middle)
    packed[0] = (unit * gains[1:2, :]).astype(bf16)


def front(line, side, far, own_rows, own_normed, own_done, seg_col, seg_row, gains, w_in, w_out):
    span, width = own_rows.shape
    rows = 2 * span
    return line.call(
        front_kernel,
        "front",
        [
            shaped((rows, 3 * width // 2), bf16),
            shaped((3, rows, width), bf16),
            shaped((rows, width), f32),
            shaped((rows, width), bf16),
            shaped((16, rows), f32),
        ],
        scratch=[pltpu.VMEM((rows, 3 * width), bf16), pltpu.VMEM((rows, rows), f32)],
        small=1,
        room=5,
    )(side, far, own_rows, own_normed, own_done, seg_col, seg_row, gains, w_in, w_out)


def plane(message, at, side):
    span = 2 * LANES
    width = message.shape[1] // 2
    start = (2 + at) * span
    return message.at[start : start + span, side * width : (side + 1) * width]


def up_kernel(packed, hot, hot_row, own_cot, far_cot, weight, message, slope_ref, masked):
    _, rows, width = packed.shape
    span, hidden = rows // 2, weight.shape[2]
    masked_rows(masked, packed[0], hot)
    message[:span, hidden:] = own_cot[...]
    message[span:rows, hidden:] = far_cot[...]
    message[rows:, :] = jnp.zeros_like(message[rows:, :])
    message[rows : rows + 8, :rows] = hot_row[...].astype(bf16)
    for n in range(0, hidden, CHUNK):
        part = weight[:, :, n : n + CHUNK].reshape(EXPERTS * width, CHUNK)
        upward = dot(masked[...], part)
        half = 0.5 * (1.0 + lax.erf(upward * ROOT_HALF))
        message[:rows, n : n + CHUNK] = (upward * half).astype(bf16)
        slope_ref[:, n : n + CHUNK] = half + upward * INV_ROOT_TAU * jnp.exp(-0.5 * upward * upward)


def up_forward(line, packed, hot, hot_row, own_cot, far_cot, weight):
    _, rows, width = packed.shape
    hidden = weight.shape[2]
    return line.call(
        up_kernel,
        "up_forward",
        [shaped((rows + 16, hidden + width), bf16), shaped((rows, hidden), f32)],
        scratch=[pltpu.VMEM((rows, EXPERTS * width), bf16)],
        room=5,
    )(packed, hot, hot_row, own_cot, far_cot, weight)


def grad_upward_kernel(far_cot, packed, hot, weight, slope, own_grad, out_ref, masked):
    rows = hot.shape[0]
    span = rows // 2
    masked_rows(masked, far_cot[...], hot[span:, :])
    for half in range(2):
        for at in range(3):
            plane(out_ref, at, half)[...] = packed[at, half * span : (half + 1) * span, :]

    def store(columns, total):
        out_ref[:span, columns] = own_grad[:, columns]
        out_ref[span:rows, columns] = (total * slope[span:, columns]).astype(bf16)

    grad_active_of(store, masked, weight)


def grad_upward_of(line, far_cot, packed, hot, weight, slope, own_grad):
    _, rows, width = packed.shape
    hidden = weight.shape[1]
    return line.call(
        grad_upward_kernel,
        "grad_upward",
        [shaped((5 * rows // 2, hidden), bf16)],
        scratch=[pltpu.VMEM((rows // 2, EXPERTS * width), bf16)],
        room=5,
    )(far_cot, packed, hot, weight, slope, own_grad)


def shortened(rows, count):
    return min(rows // 2, -(-count // 16) * 16)


def half_normed(masked, weight, out_ref):
    hidden, size, wide = weight.shape[2], out_ref.shape[0], 256
    for n in range(0, out_ref.shape[1], wide):
        total = dot(masked[:, :hidden], weight[0, n : n + wide, :], NT)
        for e in range(1, EXPERTS):
            total += dot(masked[:, e * hidden : (e + 1) * hidden], weight[e, n : n + wide, :], NT)
        out_ref[:, n : n + wide] = total[:size].astype(bf16)


def own_normed_kernel(own_active, slope, hot, weight, grad_ref, out_ref, masked):
    span = own_active.shape[0]
    grad_ref[...] = (own_active[...] * slope[:span, :]).astype(bf16)
    masked_rows(masked, grad_ref[...], hot[:span, :])
    half_normed(masked, weight, out_ref)


def own_normed_of(line, own_active, slope, hot, weight, size):
    span, hidden = own_active.shape
    return line.call(
        own_normed_kernel,
        "own_normed",
        [shaped((span, hidden), bf16), shaped((size, weight.shape[1]), bf16)],
        scratch=[pltpu.VMEM((span, EXPERTS * hidden), bf16)],
        room=5,
    )(own_active, slope, hot, weight)


def far_normed_kernel(message, hot, weight, out_ref, masked):
    rows = hot.shape[0]
    masked_rows(masked, message[rows // 2 : rows, :], hot[rows // 2 :, :])
    half_normed(masked, weight, out_ref)


def far_normed_of(line, message, hot, weight, size):
    rows, hidden = hot.shape[0], weight.shape[2]
    return line.call(
        far_normed_kernel,
        "far_normed",
        [shaped((size, weight.shape[1]), bf16)],
        scratch=[pltpu.VMEM((rows // 2, EXPERTS * hidden), bf16)],
        room=5,
    )(message, hot, weight)


def branch_kernel(sent, hot, weight, own_ref, send_ref, masked):
    rows, hidden = hot.shape[0], weight.shape[1]
    size, width = own_ref.shape
    masked_rows(masked, sent[:rows, :hidden], hot)
    wide = 256
    for n in range(0, width, wide):
        columns = slice(n, n + wide)
        total = dot(masked[:, :hidden], weight[0, :, columns])
        for e in range(1, EXPERTS):
            total += dot(masked[:, e * hidden : (e + 1) * hidden], weight[e, :, columns])
        own_ref[:, columns] = total[:size].astype(bf16)
        send_ref[:, columns] = total[rows // 2 : rows // 2 + size].astype(bf16)


def branch_of(line, sent, hot, weight, size):
    rows, (_, hidden, width) = hot.shape[0], weight.shape
    shape = shaped((size, width), bf16)
    return line.call(
        branch_kernel,
        "branch",
        [shape, shape],
        scratch=[pltpu.VMEM((rows, EXPERTS * hidden), bf16)],
        room=5,
    )(sent, hot, weight)


def masked_turned(order, rows, hot, target, part):
    turned = dot(order[...], rows, NT)
    for e in range(EXPERTS):
        target[e, :, part] = (turned * hot[e : e + 1, part].astype(f32)).astype(bf16)


def picked_grads_kernel(order, hot_own, own, far, own_ref, far_ref):
    rows, width = own_ref.shape[2], order.shape[1]
    hidden = own.shape[1] - width
    every = slice(0, rows)
    masked_turned(order, own[:rows, hidden:], hot_own, own_ref, every)
    masked_turned(order, far[:rows, hidden:], far.at[rows:, :], far_ref, every)


def picked_grads(line, order, hot_own, own, far):
    shape = shaped((EXPERTS, order.shape[0], hot_own.shape[1]), bf16)
    return line.call(picked_grads_kernel, "picked", [shape, shape])(order, hot_own, own, far)


def picked_kernel(order, hot_own, first, own, far, own_ref, far_ref):
    rows = own_ref.shape[2]
    span = rows // 2
    for source, hot, target in ((own, hot_own, own_ref), (far, first.at[rows:, :], far_ref)):
        for half in range(2):
            part = slice(half * span, (half + 1) * span)
            masked_turned(order, plane(source, 0, half)[...], hot, target, part)


def picked(line, order, hot_own, first, own, far):
    shape = shaped((EXPERTS, order.shape[0], hot_own.shape[1]), bf16)
    return line.call(picked_kernel, "picked", [shape, shape])(order, hot_own, first, own, far)


def turned_kernel(order, own, far, out_ref):
    span = out_ref.shape[2] // 2
    for at, (source, part) in enumerate(((own, 1), (far, 1), (own, 2), (far, 2))):
        for half in range(2):
            turned = dot(order[...], plane(source, part, half)[...], NT)
            out_ref[at, :, half * span : (half + 1) * span] = turned.astype(bf16)


def turned(line, order, own, far, rows):
    shape = shaped((4, order.shape[0], rows), bf16)
    return line.call(turned_kernel, "turned", [shape])(order, own, far)


def split_store(first, value, columns, keep_ref, send_ref):
    value = value.astype(bf16)
    half, quarter = value.shape[0] // 2, value.shape[0] // 4
    if first == NEAR:
        keep_ref[:, columns] = value[:half]
        send_ref[:, columns] = value[half:]
    else:
        for part in range(2):
            rows = slice(part * quarter, (part + 1) * quarter)
            keep_ref[rows, columns] = value[part * half : part * half + quarter]
            send_ref[rows, columns] = value[part * half + quarter : (part + 1) * half]


def expert_grad_kernel(first, start, stop, a_own, a_far, own, far, keep_ref, send_ref):
    rows = a_own.shape[2]
    for n in range(start, stop, CHUNK):
        wide = min(CHUNK, stop - n)
        for e in range(EXPERTS):
            both = dot(a_own[e], own[:rows, n : n + wide]) + dot(a_far[e], far[:rows, n : n + wide])
            at = e * (stop - start) + n - start
            split_store(first, both, slice(at, at + wide), keep_ref, send_ref)


def expert_grad(line, first, sides, own, far, start, stop):
    shape = shaped((sides[0].shape[1] // 2, EXPERTS * (stop - start)), bf16)
    return line.call(
        functools.partial(expert_grad_kernel, first, start, stop),
        "expert_grad",
        [shape, shape],
        room=4,
    )(*sides, own, far)


def attention_grad_kernel(first, order, sides, g_own, g_far, keep_ref, send_ref):
    rows, span = sides.shape[2], g_own.shape[1]
    for at in range(4):
        part = slice(at * rows, (at + 1) * rows)
        pair = 0 if at < 3 else 2
        both = dot(sides[pair], g_own[part, :]) + dot(sides[pair + 1], g_far[part, :])
        split_store(first, both, slice(at * span, (at + 1) * span), keep_ref, send_ref)
    sums = g_own[4 * rows : 4 * rows + 16, :].astype(f32)
    sums += g_far[4 * rows : 4 * rows + 16, :].astype(f32)
    both = dot(order[:, :span], sums[0:8].astype(bf16), NT)
    both += dot(order[:, span:], sums[8:16].astype(bf16), NT)
    tail = jnp.concatenate([both, jnp.zeros((both.shape[0], LANES - 8), f32)], axis=1)
    split_store(first, tail, slice(4 * span, 4 * span + LANES), keep_ref, send_ref)


def attention_grad(line, first, order, sides, g_own, g_far):
    shape = shaped((order.shape[0] // 2, 4 * g_own.shape[1] + LANES), bf16)
    return line.call(
        functools.partial(attention_grad_kernel, first), "attention_grad", [shape, shape]
    )(order, sides, g_own, g_far)


def weights_kernel(side, mine_ref, lse, seg_row, seg_col, out_ref, bias):
    rows, own = mine_ref.shape[0], mine_ref.shape[1] // 3
    allowed = (seg_col[:, 0:1] == 0) | (seg_col[:, 0:1] == seg_row[0:1, :])
    bias[...] = jnp.where(allowed, 0.0, NEGATIVE)
    first = lax.broadcasted_iota(jnp.int32, (rows, LANES), 1) < HEAD_DIM
    on_side = side[0] == 0
    for at in range(own // HEAD_DIM):
        columns = slice(at // 2 * LANES, (at // 2 + 1) * LANES)
        queries = mine_ref[:, columns] * jnp.asarray(SCALE, bf16)
        keys = mine_ref[:, own + at // 2 * LANES : own + (at // 2 + 1) * LANES]
        mine = first if at % 2 == 0 else ~first
        far_at = at + own // HEAD_DIM
        lse_row = jnp.where(on_side, lse[at : at + 1, :], lse[far_at : far_at + 1, :])
        scores = dot(keys, jnp.where(mine, queries, jnp.zeros_like(queries)), NT) * LOG2_E
        out_ref[at] = jnp.exp2(scores + bias[...] - lse_row).astype(bf16)


def weights_of(line, side, mine, lse, seg_row, seg_col):
    rows, three = mine.shape
    return line.call(
        weights_kernel,
        "weights",
        [shaped((three // 3 // HEAD_DIM, rows, rows), bf16)],
        scratch=[pltpu.VMEM((rows, rows), f32)],
        small=1,
        room=5,
    )(side, mine, lse, seg_row, seg_col)


def back_kernel(
    side, w_in, w_out, part_own, part_rest, far_own, far_rest, own_cot, far_cot, middle, low_rows, gains,
    mine_ref, weights, message, gm_ref, gn_ref, gn_send, branch_low, attended_back,
):
    rows, width = middle.shape
    span, own = rows // 2, width // 2
    size = gn_send.shape[0]
    start = side[0] * own
    unit, scale = layer_norm_parts(middle[...])
    blank = jnp.zeros((span - size, width), f32)
    first = part_own[...].astype(f32) + far_rest[...].astype(f32)
    second = part_rest[...].astype(f32) + far_own[...].astype(f32)
    grad = jnp.concatenate([first, blank, second, blank], axis=0)
    gains_two = jnp.sum(grad * unit, axis=0, keepdims=True)
    grads_low = jnp.concatenate([own_cot[...], far_cot[...]], axis=0)
    grad_middle = grads_low.astype(f32) + layer_norm_back(grad, gains[1:2, :], unit, scale)
    gm_ref[...] = grad_middle[:span]
    branch_low[...] = grad_middle.astype(bf16)
    out_rows = pl.ds(pl.multiple_of(start, LANES), own)
    attended_back[...] = dot(branch_low[...], w_out[out_rows, :], NT).astype(bf16)
    first = lax.broadcasted_iota(jnp.int32, (rows, LANES), 1) < HEAD_DIM
    top = lax.broadcasted_iota(jnp.int32, (LANES, rows), 0) < HEAD_DIM
    for p in range(own // LANES):
        columns = slice(p * LANES, (p + 1) * LANES)
        queries = mine_ref[:, columns] * jnp.asarray(SCALE, bf16)
        keys = mine_ref[:, own + p * LANES : own + (p + 1) * LANES]
        values = mine_ref[:, 2 * own + p * LANES : 2 * own + (p + 1) * LANES]
        grads = attended_back[:, columns]
        keys_up = jnp.transpose(keys)
        parts = []
        for head in range(2):
            mine = first if head == 0 else jnp.logical_not(first)
            low_probs = weights[2 * p + head]
            probs = low_probs.astype(f32)
            dprobs = dot(values, jnp.where(mine, grads, jnp.zeros_like(grads)), NT)
            delta = jnp.sum(probs * dprobs, axis=0, keepdims=True)
            dscores = (probs * (dprobs - delta)).astype(bf16)
            parts.append(
                (
                    dot(keys_up, dscores) * SCALE,
                    dot(dscores, queries),
                    dot(low_probs, grads),
                )
            )
        turned_back = jnp.where(top, parts[0][0], parts[1][0])
        message[0:rows, columns] = jnp.transpose(turned_back).astype(bf16)
        for at in range(1, 3):
            message[at * rows : (at + 1) * rows, columns] = jnp.where(
                first, parts[0][at], parts[1][at]
            ).astype(bf16)
    message[3 * rows : 4 * rows, :] = branch_low[:, pl.ds(pl.multiple_of(start, LANES), own)]
    grad_normed = jnp.zeros((rows, width), f32)
    for at in range(3):
        columns = pl.ds(pl.multiple_of(at * width + start, LANES), own)
        grad_normed += dot(message[at * rows : (at + 1) * rows, :], w_in[:, columns], NT)
    gn_ref[...] = grad_normed[:span]
    gn_send[...] = grad_normed[span : span + size].astype(bf16)
    unit, _ = layer_norm_parts(low_rows[...].astype(f32))
    gains_one = jnp.sum(grad_normed * unit, axis=0, keepdims=True)
    blank = jnp.zeros((6, own), f32)
    message[4 * rows :, :] = jnp.concatenate(
        [
            gains_one[:, :own], gains_two[:, :own], blank,
            gains_one[:, own:], gains_two[:, own:], blank,
        ],
        axis=0,
    ).astype(bf16)


def back(
    line, side, w_in, w_out, part_own, part_rest, far_own, far_rest, own_cot, far_cot, middle, low_rows, gains,
    mine, weights,
):
    rows, width = middle.shape
    own, span, size = width // 2, rows // 2, part_own.shape[0]
    return line.call(
        back_kernel,
        "back",
        [
            shaped((4 * rows + 16, own), bf16),
            shaped((span, width), f32),
            shaped((span, width), f32),
            shaped((size, width), bf16),
        ],
        scratch=[
            pltpu.VMEM((rows, width), bf16),
            pltpu.VMEM((rows, own), bf16),
        ],
        small=1,
        room=7,
    )(
        side, w_in, w_out, part_own, part_rest, far_own, far_rest, own_cot, far_cot, middle, low_rows, gains,
        mine, weights,
    )


def last_kernel(gm, gn, gn_far, low_rows, gains, middle, branch, branch_far, out_ref, layer_ref):
    count, size = out_ref.shape[0], gn_far.shape[0]
    unit, scale = layer_norm_parts(low_rows[:size, :].astype(f32))
    grad = gn[:size, :] + gn_far[...].astype(f32)
    total = gm[:size, :] + layer_norm_back(grad, gains[0:1, :], unit, scale)
    out_ref[...] = total[:count].astype(bf16)
    total = middle[:size, :] + branch[...].astype(f32) + branch_far[...].astype(f32)
    layer_ref[...] = total[:count].astype(bf16)


def last(line, gm, gn, gn_far, low_rows, gains, middle, branch, branch_far, count):
    shape = shaped((count, gm.shape[1]), bf16)
    return line.call(last_kernel, "last", [shape, shape], leaves=True)(
        gm, gn, gn_far, low_rows, gains, middle, branch, branch_far
    )


def add_kernel(*refs):
    keep_ref, send_ref = refs[-2:]
    half, at = keep_ref.shape[0], 0
    for keep, far in zip(refs[0:-2:2], refs[1:-2:2]):
        columns = slice(at, at + keep.shape[1])
        total = keep[...].astype(f32) + far[...].astype(f32)
        keep_ref[:, columns] = total[:half].astype(bf16)
        send_ref[:, columns] = total[half:].astype(bf16)
        at += keep.shape[1]


def added(line, pairs):
    count, wide = pairs[0][0].shape[0], sum(pair[0].shape[1] for pair in pairs)
    shape = shaped((count // 2, wide), bf16)
    return line.call(add_kernel, "added", [shape, shape])(*[v for pair in pairs for v in pair])


def finish_kernel(places, *refs):
    out_ref, start = refs[-1], 0
    for (pair, at, wide) in places:
        keep, far = refs[2 * pair], refs[2 * pair + 1]
        for e in range(EXPERTS):
            columns = slice(at + e * wide, at + (e + 1) * wide)
            out_ref[e, :, start : start + wide] = keep[:, columns].astype(f32) + far[:, columns].astype(f32)
        start += wide


def finished(line, pairs, places):
    shape = (EXPERTS, pairs[0][0].shape[0], sum(place[2] for place in places))
    kernel = functools.partial(finish_kernel, places)
    return line.call(kernel, "finished", [shaped(shape, f32)], leaves=True)(
        *[v for pair in pairs for v in pair]
    )[0]


def summed_kernel(at, keep, far, out_ref, low_ref):
    columns = slice(at, at + out_ref.shape[1])
    total = keep[:, columns].astype(f32) + far[:, columns].astype(f32)
    out_ref[...] = total
    low_ref[...] = total.astype(bf16)


def summed(line, keep, far, at, wide):
    shape = (keep.shape[0], wide)
    return line.call(
        functools.partial(summed_kernel, at), "summed", [shaped(shape, f32), shaped(shape, bf16)]
    )(keep, far)


def joined_kernel(side, own, far, in_ref, out_ref, gain_ref):
    half = out_ref.shape[1] // 2
    on_side = side[0] == 0
    for at in range(4):
        columns = slice(at * half, (at + 1) * half)
        mine, theirs = own[:, columns], far[:, columns].astype(f32)
        target, start = (in_ref, 2 * at * half) if at < 3 else (out_ref, 0)
        target[:, start : start + half] = jnp.where(on_side, mine, theirs)
        target[:, start + half : start + 2 * half] = jnp.where(on_side, theirs, mine)
    both = own[:, 4 * half :] + far[:, 4 * half :].astype(f32)
    kind = lax.broadcasted_iota(jnp.int32, both.shape, 1)
    gain_ref[...] = jnp.where(kind == 0, both, own[:, 4 * half :])


def joined(line, side, own, far):
    count, wide = own.shape
    half = (wide - LANES) // 4
    return line.call(
        joined_kernel,
        "joined",
        [shaped((count, 6 * half), f32), shaped((count, 2 * half), f32), shaped((count, LANES), f32)],
        small=1,
        leaves=True,
    )(side, own, far)


def body(
    tokens,
    segment_ids,
    expert_ids,
    norm_first,
    project_in,
    project_out,
    norm_second,
    up_weight,
    down_weight,
    cotangent,
):
    own_count, width = tokens.shape[1], tokens.shape[2]
    side = lax.axis_index("blk").astype(jnp.int32)[None]
    count = lax.axis_size("dp")
    place = (lax.axis_index("dp") % INNER).astype(jnp.int32)[None]
    outer = count // INNER
    deep = width // count
    line = Line()

    own_tokens, own_grads = tokens[0], cotangent[0]
    far_tokens = across_blk(own_tokens)
    (
        seg_col, seg_row, hot, hot_row, order, gains, own_rows, own_normed, own_cot, own_done,
        own_active, w_in, w_down, w_up, w_out,
    ) = begin(
        line, place, side, segment_ids, expert_ids, own_tokens, own_grads, norm_first, norm_second,
        (project_in, down_weight, up_weight, project_out), deep, outer,
    )
    far_cot = across_blk(own_cot)
    rows = hot.shape[0]
    size = shortened(rows, own_count)
    mine, packed, middle, low_rows, lse = front(
        line, side, far_tokens, own_rows, own_normed, own_done, seg_col, seg_row, gains, w_in, w_out
    )
    line.step = "active"
    sent, slope = up_forward(line, packed, hot, hot_row, own_cot, far_cot, w_up)
    sent_far = across_dp(sent, CORE)

    def over_outer(value, axis):
        if outer == 1:
            return value
        groups = [[o * INNER + i for o in range(outer)] for i in range(INNER)]
        return lax.psum_scatter(
            value, "dp", scatter_dimension=axis, tiled=True, axis_index_groups=groups
        )

    state, made, places = {}, {}, {}

    def send(name, axis, keep, going):
        state[name] = (keep, across_dp(going, axis))

    for step in STEPS:
        line.step = step
        if step[0] == "+":
            send(step[1:], PIECES[step[1:]][1][1], *added(line, [state[step[1:]]]))
        elif step[0] == "=":
            (group,) = [names for names in GROUPS if names[0] == step[1:]]
            at = 0
            for name in group:
                places[name] = (step, at)
                at += state[name][0].shape[1]
            send(step, FAR, *added(line, [state[name] for name in group]))
        elif step == "in":
            axis = PIECES[step][1][0]
            send(step, axis, *attention_grad(line, axis, order, sides, message, message_far))
        elif step in PIECES:
            (start, stop), (axis, _) = PIECES[step]
            pair = (later, later_far) if step[0] == "u" else (sent, sent_far)
            send(step, axis, *expert_grad(line, axis, made[step[0]], *pair, start * UNIT, stop * UNIT))
        elif step == "gu":
            (later,) = grad_upward_of(line, far_cot, packed, hot, w_down, slope, own_grad)
            later_far = across_dp(later, CORE)
        elif step == "half":
            own_grad, part_own = own_normed_of(line, own_active, slope, hot, w_up, size)
            far_own = across_blk(part_own)
        elif step == "rest":
            (part_rest,) = far_normed_of(line, later, hot, w_up, size)
            far_rest = across_blk(part_rest)
        elif step == "weights":
            (weights,) = weights_of(line, side, mine, lse, seg_row, seg_col)
        elif step == "branch":
            branch, branch_send = branch_of(line, sent, hot, w_down, size)
            branch_far = across_blk(branch_send)
        elif step == "cot":
            made["d"] = picked_grads(line, order, hot_row, sent, sent_far)
        elif step == "two":
            made["u"] = picked(line, order, hot_row, sent_far, later, later_far)
        elif step == "pick":
            (sides,) = turned(line, order, later, later_far, rows)
        elif step == "back":
            message, gm_own, gn_own, gn_send = back(
                line, side, w_in, w_out, part_own, part_rest, far_own, far_rest, own_cot,
                far_cot, middle, low_rows, gains, mine, weights,
            )
            message_far = across_dp(message, CORE)
            gn_far = across_blk(gn_send)
        elif step == "last":
            input_grad, layer_out = last(
                line, gm_own, gn_own, gn_far, low_rows, gains, middle, branch, branch_far, own_count
            )
        elif step in ("down", "up"):
            names = sorted(n for n in PIECES if n[0] == step[0])
            groups = sorted({places[n][0] for n in names})
            cut = [
                (groups.index(places[n][0]), places[n][1], (PIECES[n][0][1] - PIECES[n][0][0]) * UNIT)
                for n in names
            ]
            made[step] = finished(line, [state[g] for g in groups], cut)
        elif step == "sum":
            wide = 2 * width + LANES
            in_sum, in_low = summed(line, *state[places["in"][0]], places["in"][1], wide)
            if outer > 1:
                in_sum = over_outer(in_sum, 0)
                in_low = in_sum.astype(bf16)
            in_far = across_blk(in_low)
        elif step == "join":
            in_out, out_out, gain_out = joined(line, side, in_sum, in_far)

    up_out = over_outer(made["up"], 1)
    down_out = over_outer(made["down"], 1).transpose(0, 2, 1)
    return (
        layer_out[None],
        input_grad[None],
        gain_out[:, 0],
        in_out,
        out_out,
        gain_out[:, 1],
        up_out,
        down_out,
    )


def solution(mesh):
    return jax.shard_map(
        body,
        mesh=mesh,
        in_specs=(
            P("dp", "blk", None),
            P("dp", None),
            P("dp", None),
            P(),
            P(),
            P(),
            P(),
            P(None, None, "blk"),
            P(None, "blk", None),
            P("dp", "blk", None),
        ),
        out_specs=(
            P("dp", "blk", None),
            P("dp", "blk", None),
            P("dp"),
            P("dp", None),
            P("dp", None),
            P("dp"),
            P(None, "dp", "blk"),
            P(None, "blk", "dp"),
        ),
        check_vma=False,
    )
```

```python
import functools

import jax
import jax.numpy as jnp
import numpy as np
from jax import lax
from jax.experimental import pallas as pl
from jax.experimental.pallas import tpu as pltpu
from jax.sharding import PartitionSpec as P

HEAD_DIM = 64
EXPERTS = 3
EPSILON = 1e-05
NEGATIVE = -1e30
ROOT_HALF = 0.7071067811865476
INV_ROOT_TAU = 0.3989422804014327
SCALE = HEAD_DIM ** (-0.5)
LOG2_E = 1.4426950408889634
LANES = 128
CHUNK = 512
UNIT = 256
INNER = 16
CORE, NEAR, MID, FAR = 1, 2, 4, 8
COSTS = {'down': 3, 'last': 60, 'half': 10}
HELD_BACK = {
    None: 1, "active": 2, "half": 6, "gu": 12, "cot": 13, "d0": 14, "d1": 18, "rest": 23, "two": 24,
    "pick": 25, "u3": 27, "weights": 28, "back": 30, "+d1": 30, "+d0": 30, "in": 31, "u2": 33, "branch": 36,
    "=d0": 36, "+u3": 42, "+in": 42, "u0": 44, "last": 45, "+u2": 45, "=in": 45, "u1": 48, "+u0": 48,
    "=u2": 48, "down": 48, "+u1": 48, "sum": 48, "=u0": 48, "join": 48, "=u1": 48, "up": 48,
}

PIECES = {
    "d0": ((0, 4), (MID, NEAR)),
    "d1": ((4, 6), (NEAR, MID)),
    "u0": ((0, 1), (NEAR, MID)),
    "u1": ((1, 2), (NEAR, MID)),
    "u2": ((2, 4), (NEAR, MID)),
    "u3": ((4, 6), (NEAR, MID)),
    "in": (None, (MID, NEAR)),
}
GROUPS = (("in",), ("d0", "d1"), ("u2", "u3"), ("u0",), ("u1",))
STEPS = (
    "half", "gu", "cot", "d0", "d1", "two", "rest", "pick", "u3", "weights", "back", "+d0", "+d1", "in", "u2",
    "branch", "=d0", "+u3", "+in", "u0", "last", "+u2", "=in", "u1", "+u0", "=u2", "down", "+u1", "sum", "=u0",
    "join", "=u1", "up",
)

f32 = jnp.float32
bf16 = jnp.bfloat16

NN = ((1,), (0,))
NT = ((1,), (1,))


def across_blk(value):
    return lax.ppermute(value, "blk", [(0, 1), (1, 0)])


def across_dp(value, bit):
    count = lax.axis_size("dp")
    return lax.ppermute(value, "dp", [(source, source ^ bit) for source in range(count)])


def dot(a, b, dims=NN):
    return lax.dot_general(a, b, (dims, ((), ())), preferred_element_type=f32)


def layer_norm_parts(values):
    row_mean = jnp.mean(values, axis=-1, keepdims=True)
    centred = values - row_mean
    row_var = jnp.mean(centred * centred, axis=-1, keepdims=True)
    scale = lax.rsqrt(row_var + EPSILON)
    return centred * scale, scale


def layer_norm_back(grad, gain, unit, scale):
    raised = grad * gain
    return scale * (
        raised
        - jnp.mean(raised, axis=-1, keepdims=True)
        - unit * jnp.mean(raised * unit, axis=-1, keepdims=True)
    )


def shaped(shape, dtype):
    return jax.ShapeDtypeStruct(shape, dtype)


def held(shape, dtype):
    size = np.dtype(dtype).itemsize
    shape = (1,) * (2 - len(shape)) + tuple(shape)
    lead = int(np.prod(shape[:-2])) if len(shape) > 2 else 1
    return lead * -(-shape[-2] // 16) * 16 * -(-shape[-1] // LANES) * LANES * size


class Line:
    def __init__(self):
        self.last, self.step = None, None

    def call(self, kernel, name, outs, scratch=(), small=0, large=0, room=3, leaves=False):
        def run(*operands):
            count, total = len(operands), len(outs)
            need = sum(held(v.shape, v.dtype) for v in scratch if v.memory_space == pltpu.VMEM)
            if leaves:
                need += sum(held(v.shape, v.dtype) for v in outs)
                results = list(outs)
            else:
                results = [pltpu.VMEM(v.shape, v.dtype) for v in outs]
            whole = pl.BlockSpec(memory_space=pltpu.VMEM)
            far = pl.BlockSpec(memory_space=pltpu.HBM)
            specs = [pl.BlockSpec(memory_space=pltpu.SMEM)] * small + [far] * large
            specs += [whole] * (count - small - large)
            places = [None] * small + [pltpu.HBM] * large + [pltpu.VMEM] * (count - small - large)
            operands = tuple(
                v if place is None else pltpu.with_memory_space_constraint(v, place)
                for v, place in zip(operands, places)
            )
            if self.last is not None:
                operands += (pltpu.with_memory_space_constraint(self.last, pltpu.HBM),)
                specs.append(far)
            first = len(operands)

            def body_of(*refs):
                kernel(*refs[:count], *refs[first : first + total], *refs[first + total + 1 :])

            *result, self.last = pl.pallas_call(
                body_of,
                name=name,
                out_shape=[*results, pltpu.HBM((HELD_BACK.get(self.step, HELD_BACK[None]) * 2048, LANES), f32)],
                in_specs=specs,
                out_specs=[whole] * total + [far],
                scratch_shapes=list(scratch),
                compiler_params=pltpu.CompilerParams(vmem_limit_bytes=need + room * 2**20),
                cost_estimate=pl.CostEstimate(
                    flops=COSTS.get(self.step, 10) * 10**9, bytes_accessed=1000, transcendentals=0
                ),
            )(*operands)
            return result

        return run


def masked_rows(target, value, hot):
    span = value.shape[1]
    for e in range(EXPERTS):
        target[:, e * span : (e + 1) * span] = value * hot[:, e : e + 1]


def grad_active_of(target, masked, weight):
    width, hidden = weight.shape[2], weight.shape[1]
    for n in range(0, hidden, CHUNK):
        total = dot(masked[:, :width], weight[0, n : n + CHUNK, :], NT)
        for e in range(1, EXPERTS):
            total += dot(masked[:, e * width : (e + 1) * width], weight[e, n : n + CHUNK, :], NT)
        target(slice(n, n + CHUNK), total)


def begin_kernel(
    deep, outer, place, side, ids_hbm, experts_hbm, tokens_hbm, grads_hbm, one_hbm, two_hbm,
    w_in_hbm, down_hbm, up_hbm, w_out_hbm,
    bias, hot, hot_row, order, gains, own_rows, own_normed, own_cot, cot_sent, projected,
    grad_active, w_in, down, up, w_out,
    ids, experts, tokens, grads, one, two, masked, sems,
):
    pairs = (
        (ids_hbm, ids), (experts_hbm, experts), (tokens_hbm, tokens), (one_hbm, one),
        (grads_hbm, grads), (two_hbm, two), (w_in_hbm, w_in), (down_hbm, down),
        (up_hbm, up), (w_out_hbm, w_out),
    )
    copies = [pltpu.make_async_copy(a, b, sems.at[at]) for at, (a, b) in enumerate(pairs)]
    for copy in copies:
        copy.start()
    rows, (count, width) = hot.shape[0], tokens.shape
    span = rows // 2
    on_side = side[0] == 0
    step = outer * deep
    lane = lax.broadcasted_iota(jnp.int32, (step, width), 1)
    low = lax.broadcasted_iota(jnp.int32, (step, width), 0)
    skip = low
    for late in range(1, outer):
        skip += jnp.where(low >= late * deep, (INNER - 1) * deep, 0)
    for block in range(INNER // 2):
        relative = ((block >> 2) & 1) * NEAR + ((block >> 1) & 1) * MID + (block & 1) * FAR
        base = (place[0] ^ relative) * deep
        order[block * step : (block + 1) * step, :] = (lane - base == skip).astype(f32).astype(bf16)
    for copy in copies[:6]:
        copy.wait()

    def both(values):
        halves = values[0:1, :count], values[0:1, count:]
        pad = jnp.full((1, span - count), -1, jnp.int32)
        first = jnp.where(on_side, halves[0], halves[1])
        second = jnp.where(on_side, halves[1], halves[0])
        return jnp.broadcast_to(jnp.concatenate([first, pad, second, pad], axis=1), (8, rows))

    segments, expert = both(ids), both(experts)
    keys = jnp.transpose(segments)[:, 0:1]
    bias[...] = jnp.where((keys == 0) | (keys == segments[0:1, :]), 0.0, NEGATIVE)
    hot_row[...] = (lax.broadcasted_iota(jnp.int32, (8, rows), 0) == expert).astype(f32)
    hot[...] = (lax.broadcasted_iota(jnp.int32, (rows, 8), 1) == jnp.transpose(expert)).astype(bf16)
    gains[...] = jnp.zeros_like(gains)
    gains[0:1, :] = one[...].reshape(1, width)
    gains[1:2, :] = two[...].reshape(1, width)
    own_cot[...] = jnp.zeros_like(own_cot)
    own_cot[0:count, :] = grads[...]
    cot_sent[...] = own_cot[: cot_sent.shape[0], :]
    own_rows[...] = jnp.zeros_like(own_rows)
    own_rows[0:count, :] = tokens[...]
    unit, _ = layer_norm_parts(own_rows[...].astype(f32))
    normed = (unit * gains[0:1, :]).astype(bf16)
    own_normed[...] = normed
    copies[6].wait()
    projected[...] = dot(normed, w_in[...]).astype(bf16)
    masked_rows(masked, own_cot[...], hot[:span, :])
    copies[7].wait()

    def store(columns, total):
        grad_active[:, columns] = total

    grad_active_of(store, masked, down)
    for copy in copies[8:]:
        copy.wait()


def begin(line, place, side, ids, experts, tokens, grads, one, two, weights, deep, outer):
    count, width = tokens.shape
    hidden = weights[1].shape[1]
    span = -(-count // LANES) * LANES
    rows = 2 * span
    inside = (ids, experts, tokens, grads, one, two)
    return line.call(
        functools.partial(begin_kernel, deep, outer),
        "begin",
        [
            shaped((rows, rows), f32),
            shaped((rows, 8), bf16),
            shaped((8, rows), f32),
            shaped((width // 2, width), bf16),
            shaped((8, width), f32),
            shaped((span, width), bf16),
            shaped((span, width), bf16),
            shaped((span, width), bf16),
            shaped((shortened(rows, count), width), bf16),
            shaped((span, 3 * width), bf16),
            shaped((span, hidden), f32),
            *[shaped(w.shape, w.dtype) for w in weights],
        ],
        scratch=[
            *[pltpu.VMEM(v.shape, v.dtype) for v in inside],
            pltpu.VMEM((span, EXPERTS * width), bf16),
            pltpu.SemaphoreType.DMA((10,)),
        ],
        small=2,
        large=10,
    )(place, side, *inside, *weights)


def front_kernel(
    side, far, own_rows, own_normed, own_done, bias, gains, w_in, w_out,
    mine_ref, packed, middle_ref, low_rows, lse_ref, projected,
):
    count, width = far.shape
    rows = projected.shape[0]
    span, own = rows // 2, width // 2
    low_rows[0:span, :] = own_rows[...]
    low_rows[span:, :] = jnp.zeros((span, width), bf16)
    low_rows[span : span + count, :] = far[...]
    unit, _ = layer_norm_parts(low_rows[span:, :].astype(f32))
    normed = (unit * gains[0:1, :]).astype(bf16)
    packed[1, :span, :] = own_normed[...]
    packed[1, span:, :] = normed
    projected[:span, :] = own_done[...]
    projected[span:, :] = dot(normed, w_in[...]).astype(bf16)
    first = lax.broadcasted_iota(jnp.int32, (rows, LANES), 1) < HEAD_DIM
    top = lax.broadcasted_iota(jnp.int32, (LANES, rows), 0) < HEAD_DIM
    lse_ref[...] = jnp.zeros_like(lse_ref)
    for p in range(width // LANES):
        columns = slice(p * LANES, (p + 1) * LANES)
        queries = projected[:, columns] * jnp.asarray(SCALE, bf16)
        keys = projected[:, width + p * LANES : width + (p + 1) * LANES]
        values = jnp.transpose(projected[:, 2 * width + p * LANES : 2 * width + (p + 1) * LANES])
        outs = []
        for head in range(2):
            mine, mine_up = (first, top) if head == 0 else (~first, ~top)
            scores = dot(keys, jnp.where(mine, queries, jnp.zeros_like(queries)), NT)
            scores = scores * LOG2_E + bias[...]
            peak = jnp.max(scores, axis=0, keepdims=True)
            raised = jnp.exp2(scores - peak).astype(bf16)
            summed = dot(jnp.where(mine_up, values, jnp.ones_like(values)), raised)
            at = (1 - head) * HEAD_DIM
            total = summed[at : at + 1, :]
            outs.append(summed * (1.0 / total))
            lse_ref[2 * p + head : 2 * p + head + 1, :] = peak + jnp.log2(total)
        packed[2, :, columns] = jnp.transpose(jnp.where(top, outs[0], outs[1])).astype(bf16)
    for at in range(3):
        start = pl.multiple_of(at * width + side[0] * own, LANES)
        mine_ref[:, at * own : (at + 1) * own] = projected[:, pl.ds(start, own)]
    middle = low_rows[...].astype(f32) + dot(packed[2], w_out[...])
    middle_ref[...] = middle
    unit, _ = layer_norm_parts(middle)
    packed[0] = (unit * gains[1:2, :]).astype(bf16)


def front(line, side, far, own_rows, own_normed, own_done, bias, gains, w_in, w_out):
    span, width = own_rows.shape
    rows = 2 * span
    return line.call(
        front_kernel,
        "front",
        [
            shaped((rows, 3 * width // 2), bf16),
            shaped((3, rows, width), bf16),
            shaped((rows, width), f32),
            shaped((rows, width), bf16),
            shaped((16, rows), f32),
        ],
        scratch=[pltpu.VMEM((rows, 3 * width), bf16)],
        small=1,
        room=5,
    )(side, far, own_rows, own_normed, own_done, bias, gains, w_in, w_out)


def plane(message, at, side):
    span = 2 * LANES
    width = message.shape[1] // 2
    start = (2 + at) * span
    return message.at[start : start + span, side * width : (side + 1) * width]


def up_kernel(packed, hot, hot_row, own_cot, far_cot, weight, message, slope_ref, masked):
    _, rows, width = packed.shape
    span, hidden = rows // 2, weight.shape[2]
    masked_rows(masked, packed[0], hot)
    message[:span, hidden:] = own_cot[...]
    sent = far_cot.shape[0]
    message[span : span + sent, hidden:] = far_cot[...]
    message[span + sent : rows, hidden:] = jnp.zeros((span - sent, width), bf16)
    message[rows:, :] = jnp.zeros_like(message[rows:, :])
    message[rows : rows + 8, :rows] = hot_row[...].astype(bf16)
    for n in range(0, hidden, CHUNK):
        part = weight[:, :, n : n + CHUNK].reshape(EXPERTS * width, CHUNK)
        upward = dot(masked[...], part)
        half = 0.5 * (1.0 + lax.erf(upward * ROOT_HALF))
        message[:rows, n : n + CHUNK] = (upward * half).astype(bf16)
        slope_ref[:, n : n + CHUNK] = half + upward * INV_ROOT_TAU * jnp.exp(-0.5 * upward * upward)


def up_forward(line, packed, hot, hot_row, own_cot, far_cot, weight):
    _, rows, width = packed.shape
    hidden = weight.shape[2]
    return line.call(
        up_kernel,
        "up_forward",
        [shaped((rows + 16, hidden + width), bf16), shaped((rows, hidden), f32)],
        scratch=[pltpu.VMEM((rows, EXPERTS * width), bf16)],
        room=5,
    )(packed, hot, hot_row, own_cot, far_cot, weight)


def grad_upward_kernel(far_cot, packed, hot, weight, slope, own_grad, out_ref, masked):
    rows = hot.shape[0]
    span = rows // 2
    sent = far_cot.shape[0]
    masked[sent:, :] = jnp.zeros_like(masked[sent:, :])
    masked_rows(masked.at[:sent, :], far_cot[...], hot[span : span + sent, :])
    for half in range(2):
        for at in range(3):
            plane(out_ref, at, half)[...] = packed[at, half * span : (half + 1) * span, :]

    def store(columns, total):
        out_ref[:span, columns] = own_grad[:, columns]
        out_ref[span:rows, columns] = (total * slope[span:, columns]).astype(bf16)

    grad_active_of(store, masked, weight)


def grad_upward_of(line, far_cot, packed, hot, weight, slope, own_grad):
    _, rows, width = packed.shape
    hidden = weight.shape[1]
    return line.call(
        grad_upward_kernel,
        "grad_upward",
        [shaped((5 * rows // 2, hidden), bf16)],
        scratch=[pltpu.VMEM((rows // 2, EXPERTS * width), bf16)],
        room=5,
    )(far_cot, packed, hot, weight, slope, own_grad)


def shortened(rows, count):
    return min(rows // 2, -(-count // 16) * 16)


def half_normed(masked, weight, out_ref):
    hidden, size, wide = weight.shape[2], out_ref.shape[0], 256
    for n in range(0, out_ref.shape[1], wide):
        total = dot(masked[:, :hidden], weight[0, n : n + wide, :], NT)
        for e in range(1, EXPERTS):
            total += dot(masked[:, e * hidden : (e + 1) * hidden], weight[e, n : n + wide, :], NT)
        out_ref[:, n : n + wide] = total[:size].astype(bf16)


def own_normed_kernel(own_active, slope, hot, weight, grad_ref, out_ref, masked):
    span = own_active.shape[0]
    grad_ref[...] = (own_active[...] * slope[:span, :]).astype(bf16)
    masked_rows(masked, grad_ref[...], hot[:span, :])
    half_normed(masked, weight, out_ref)


def own_normed_of(line, own_active, slope, hot, weight, size):
    span, hidden = own_active.shape
    return line.call(
        own_normed_kernel,
        "own_normed",
        [shaped((span, hidden), bf16), shaped((size, weight.shape[1]), bf16)],
        scratch=[pltpu.VMEM((span, EXPERTS * hidden), bf16)],
        room=5,
    )(own_active, slope, hot, weight)


def far_normed_kernel(message, hot, weight, out_ref, masked):
    rows = hot.shape[0]
    masked_rows(masked, message[rows // 2 : rows, :], hot[rows // 2 :, :])
    half_normed(masked, weight, out_ref)


def far_normed_of(line, message, hot, weight, size):
    rows, hidden = hot.shape[0], weight.shape[2]
    return line.call(
        far_normed_kernel,
        "far_normed",
        [shaped((size, weight.shape[1]), bf16)],
        scratch=[pltpu.VMEM((rows // 2, EXPERTS * hidden), bf16)],
        room=5,
    )(message, hot, weight)


def branch_kernel(sent, hot, weight, own_ref, send_ref, masked):
    rows, hidden = hot.shape[0], weight.shape[1]
    size, width = own_ref.shape
    masked_rows(masked, sent[:rows, :hidden], hot)
    wide = 256
    for n in range(0, width, wide):
        columns = slice(n, n + wide)
        total = dot(masked[:, :hidden], weight[0, :, columns])
        for e in range(1, EXPERTS):
            total += dot(masked[:, e * hidden : (e + 1) * hidden], weight[e, :, columns])
        own_ref[:, columns] = total[:size].astype(bf16)
        send_ref[:, columns] = total[rows // 2 : rows // 2 + size].astype(bf16)


def branch_of(line, sent, hot, weight, size):
    rows, (_, hidden, width) = hot.shape[0], weight.shape
    shape = shaped((size, width), bf16)
    return line.call(
        branch_kernel,
        "branch",
        [shape, shape],
        scratch=[pltpu.VMEM((rows, EXPERTS * hidden), bf16)],
        room=5,
    )(sent, hot, weight)


def masked_turned(order, rows, hot, target, part):
    turned = dot(order[...], rows, NT)
    for e in range(EXPERTS):
        target[e, :, part] = (turned * hot[e : e + 1, part].astype(f32)).astype(bf16)


def picked_grads_kernel(order, hot_own, own, far, own_ref, far_ref):
    rows, width = own_ref.shape[2], order.shape[1]
    hidden = own.shape[1] - width
    every = slice(0, rows)
    masked_turned(order, own[:rows, hidden:], hot_own, own_ref, every)
    masked_turned(order, far[:rows, hidden:], far.at[rows:, :], far_ref, every)


def picked_grads(line, order, hot_own, own, far):
    shape = shaped((EXPERTS, order.shape[0], hot_own.shape[1]), bf16)
    return line.call(picked_grads_kernel, "picked", [shape, shape])(order, hot_own, own, far)


def picked_kernel(order, hot_own, first, own, far, own_ref, far_ref):
    rows = own_ref.shape[2]
    span = rows // 2
    for source, hot, target in ((own, hot_own, own_ref), (far, first.at[rows:, :], far_ref)):
        for half in range(2):
            part = slice(half * span, (half + 1) * span)
            masked_turned(order, plane(source, 0, half)[...], hot, target, part)


def picked(line, order, hot_own, first, own, far):
    shape = shaped((EXPERTS, order.shape[0], hot_own.shape[1]), bf16)
    return line.call(picked_kernel, "picked", [shape, shape])(order, hot_own, first, own, far)


def turned_kernel(order, own, far, out_ref):
    span = out_ref.shape[2] // 2
    for at, (source, part) in enumerate(((own, 1), (far, 1), (own, 2), (far, 2))):
        for half in range(2):
            turned = dot(order[...], plane(source, part, half)[...], NT)
            out_ref[at, :, half * span : (half + 1) * span] = turned.astype(bf16)


def turned(line, order, own, far, rows):
    shape = shaped((4, order.shape[0], rows), bf16)
    return line.call(turned_kernel, "turned", [shape])(order, own, far)


def split_store(first, value, columns, keep_ref, send_ref):
    value = value.astype(bf16)
    half, quarter = value.shape[0] // 2, value.shape[0] // 4
    if first == NEAR:
        keep_ref[:, columns] = value[:half]
        send_ref[:, columns] = value[half:]
    else:
        for part in range(2):
            rows = slice(part * quarter, (part + 1) * quarter)
            keep_ref[rows, columns] = value[part * half : part * half + quarter]
            send_ref[rows, columns] = value[part * half + quarter : (part + 1) * half]


def expert_grad_kernel(first, start, stop, a_own, a_far, own, far, keep_ref, send_ref):
    rows = a_own.shape[2]
    for n in range(start, stop, CHUNK):
        wide = min(CHUNK, stop - n)
        for e in range(EXPERTS):
            both = dot(a_own[e], own[:rows, n : n + wide]) + dot(a_far[e], far[:rows, n : n + wide])
            at = e * (stop - start) + n - start
            split_store(first, both, slice(at, at + wide), keep_ref, send_ref)


def expert_grad(line, first, sides, own, far, start, stop):
    shape = shaped((sides[0].shape[1] // 2, EXPERTS * (stop - start)), bf16)
    return line.call(
        functools.partial(expert_grad_kernel, first, start, stop),
        "expert_grad",
        [shape, shape],
        room=4,
    )(*sides, own, far)


def attention_grad_kernel(first, order, sides, g_own, g_far, keep_ref, send_ref):
    rows, span = sides.shape[2], g_own.shape[1]
    for at in range(4):
        part = slice(at * rows, (at + 1) * rows)
        pair = 0 if at < 3 else 2
        both = dot(sides[pair], g_own[part, :]) + dot(sides[pair + 1], g_far[part, :])
        split_store(first, both, slice(at * span, (at + 1) * span), keep_ref, send_ref)
    sums = g_own[4 * rows : 4 * rows + 16, :].astype(f32)
    sums += g_far[4 * rows : 4 * rows + 16, :].astype(f32)
    both = dot(order[:, :span], sums[0:8].astype(bf16), NT)
    both += dot(order[:, span:], sums[8:16].astype(bf16), NT)
    tail = jnp.concatenate([both, jnp.zeros((both.shape[0], LANES - 8), f32)], axis=1)
    split_store(first, tail, slice(4 * span, 4 * span + LANES), keep_ref, send_ref)


def attention_grad(line, first, order, sides, g_own, g_far):
    shape = shaped((order.shape[0] // 2, 4 * g_own.shape[1] + LANES), bf16)
    return line.call(
        functools.partial(attention_grad_kernel, first), "attention_grad", [shape, shape]
    )(order, sides, g_own, g_far)


def weights_kernel(side, mine_ref, lse, bias, out_ref):
    rows, own = mine_ref.shape[0], mine_ref.shape[1] // 3
    first = lax.broadcasted_iota(jnp.int32, (rows, LANES), 1) < HEAD_DIM
    on_side = side[0] == 0
    for at in range(own // HEAD_DIM):
        columns = slice(at // 2 * LANES, (at // 2 + 1) * LANES)
        queries = mine_ref[:, columns] * jnp.asarray(SCALE, bf16)
        keys = mine_ref[:, own + at // 2 * LANES : own + (at // 2 + 1) * LANES]
        mine = first if at % 2 == 0 else ~first
        far_at = at + own // HEAD_DIM
        lse_row = jnp.where(on_side, lse[at : at + 1, :], lse[far_at : far_at + 1, :])
        scores = dot(keys, jnp.where(mine, queries, jnp.zeros_like(queries)), NT) * LOG2_E
        out_ref[at] = jnp.exp2(scores + bias[...] - lse_row).astype(bf16)


def weights_of(line, side, mine, lse, bias):
    rows, three = mine.shape
    return line.call(
        weights_kernel,
        "weights",
        [shaped((three // 3 // HEAD_DIM, rows, rows), bf16)],
        small=1,
        room=5,
    )(side, mine, lse, bias)


def back_kernel(
    side, w_in, w_out, part_own, part_rest, far_own, far_rest, own_cot, far_cot, middle, low_rows, gains,
    mine_ref, weights, message, gm_ref, gn_ref, gn_send, branch_low, attended_back,
):
    rows, width = middle.shape
    span, own = rows // 2, width // 2
    size = gn_send.shape[0]
    start = side[0] * own
    unit, scale = layer_norm_parts(middle[...])
    blank = jnp.zeros((span - size, width), f32)
    first = part_own[...].astype(f32) + far_rest[...].astype(f32)
    second = part_rest[...].astype(f32) + far_own[...].astype(f32)
    grad = jnp.concatenate([first, blank, second, blank], axis=0)
    gains_two = jnp.sum(grad * unit, axis=0, keepdims=True)
    blank = jnp.zeros((span - size, width), bf16)
    grads_low = jnp.concatenate([own_cot[...], far_cot[...], blank], axis=0)
    grad_middle = grads_low.astype(f32) + layer_norm_back(grad, gains[1:2, :], unit, scale)
    gm_ref[...] = grad_middle[:span]
    branch_low[...] = grad_middle.astype(bf16)
    out_rows = pl.ds(pl.multiple_of(start, LANES), own)
    attended_back[...] = dot(branch_low[...], w_out[out_rows, :], NT).astype(bf16)
    first = lax.broadcasted_iota(jnp.int32, (rows, LANES), 1) < HEAD_DIM
    top = lax.broadcasted_iota(jnp.int32, (LANES, rows), 0) < HEAD_DIM
    for p in range(own // LANES):
        columns = slice(p * LANES, (p + 1) * LANES)
        queries = mine_ref[:, columns] * jnp.asarray(SCALE, bf16)
        keys = mine_ref[:, own + p * LANES : own + (p + 1) * LANES]
        values = mine_ref[:, 2 * own + p * LANES : 2 * own + (p + 1) * LANES]
        grads = attended_back[:, columns]
        keys_up = jnp.transpose(keys)
        parts = []
        for head in range(2):
            mine = first if head == 0 else jnp.logical_not(first)
            low_probs = weights[2 * p + head]
            probs = low_probs.astype(f32)
            dprobs = dot(values, jnp.where(mine, grads, jnp.zeros_like(grads)), NT)
            delta = jnp.sum(probs * dprobs, axis=0, keepdims=True)
            dscores = (probs * (dprobs - delta)).astype(bf16)
            parts.append(
                (
                    dot(keys_up, dscores) * SCALE,
                    dot(dscores, queries),
                    dot(low_probs, grads),
                )
            )
        turned_back = jnp.where(top, parts[0][0], parts[1][0])
        message[0:rows, columns] = jnp.transpose(turned_back).astype(bf16)
        for at in range(1, 3):
            message[at * rows : (at + 1) * rows, columns] = jnp.where(
                first, parts[0][at], parts[1][at]
            ).astype(bf16)
    message[3 * rows : 4 * rows, :] = branch_low[:, pl.ds(pl.multiple_of(start, LANES), own)]
    grad_normed = jnp.zeros((rows, width), f32)
    for at in range(3):
        columns = pl.ds(pl.multiple_of(at * width + start, LANES), own)
        grad_normed += dot(message[at * rows : (at + 1) * rows, :], w_in[:, columns], NT)
    gn_ref[...] = grad_normed[:span]
    gn_send[...] = grad_normed[span : span + size].astype(bf16)
    unit, _ = layer_norm_parts(low_rows[...].astype(f32))
    gains_one = jnp.sum(grad_normed * unit, axis=0, keepdims=True)
    blank = jnp.zeros((6, own), f32)
    message[4 * rows :, :] = jnp.concatenate(
        [
            gains_one[:, :own], gains_two[:, :own], blank,
            gains_one[:, own:], gains_two[:, own:], blank,
        ],
        axis=0,
    ).astype(bf16)


def back(
    line, side, w_in, w_out, part_own, part_rest, far_own, far_rest, own_cot, far_cot, middle, low_rows, gains,
    mine, weights,
):
    rows, width = middle.shape
    own, span, size = width // 2, rows // 2, part_own.shape[0]
    return line.call(
        back_kernel,
        "back",
        [
            shaped((4 * rows + 16, own), bf16),
            shaped((span, width), f32),
            shaped((span, width), f32),
            shaped((size, width), bf16),
        ],
        scratch=[
            pltpu.VMEM((rows, width), bf16),
            pltpu.VMEM((rows, own), bf16),
        ],
        small=1,
        room=7,
    )(
        side, w_in, w_out, part_own, part_rest, far_own, far_rest, own_cot, far_cot, middle, low_rows, gains,
        mine, weights,
    )


def last_kernel(gm, gn, gn_far, low_rows, gains, middle, branch, branch_far, out_ref, layer_ref):
    count, size = out_ref.shape[0], gn_far.shape[0]
    unit, scale = layer_norm_parts(low_rows[:size, :].astype(f32))
    grad = gn[:size, :] + gn_far[...].astype(f32)
    total = gm[:size, :] + layer_norm_back(grad, gains[0:1, :], unit, scale)
    out_ref[...] = total[:count].astype(bf16)
    total = middle[:size, :] + branch[...].astype(f32) + branch_far[...].astype(f32)
    layer_ref[...] = total[:count].astype(bf16)


def last(line, gm, gn, gn_far, low_rows, gains, middle, branch, branch_far, count):
    shape = shaped((count, gm.shape[1]), bf16)
    return line.call(last_kernel, "last", [shape, shape], leaves=True)(
        gm, gn, gn_far, low_rows, gains, middle, branch, branch_far
    )


def add_kernel(*refs):
    keep_ref, send_ref = refs[-2:]
    half, at = keep_ref.shape[0], 0
    for keep, far in zip(refs[0:-2:2], refs[1:-2:2]):
        columns = slice(at, at + keep.shape[1])
        total = keep[...].astype(f32) + far[...].astype(f32)
        keep_ref[:, columns] = total[:half].astype(bf16)
        send_ref[:, columns] = total[half:].astype(bf16)
        at += keep.shape[1]


def added(line, pairs):
    count, wide = pairs[0][0].shape[0], sum(pair[0].shape[1] for pair in pairs)
    shape = shaped((count // 2, wide), bf16)
    return line.call(add_kernel, "added", [shape, shape])(*[v for pair in pairs for v in pair])


def finish_kernel(places, *refs):
    out_ref, start = refs[-1], 0
    for (pair, at, wide) in places:
        keep, far = refs[2 * pair], refs[2 * pair + 1]
        for e in range(EXPERTS):
            columns = slice(at + e * wide, at + (e + 1) * wide)
            out_ref[e, :, start : start + wide] = keep[:, columns].astype(f32) + far[:, columns].astype(f32)
        start += wide


def finished(line, pairs, places):
    shape = (EXPERTS, pairs[0][0].shape[0], sum(place[2] for place in places))
    kernel = functools.partial(finish_kernel, places)
    return line.call(kernel, "finished", [shaped(shape, f32)], leaves=True)(
        *[v for pair in pairs for v in pair]
    )[0]


def summed_kernel(at, keep, far, out_ref, low_ref):
    columns = slice(at, at + out_ref.shape[1])
    total = keep[:, columns].astype(f32) + far[:, columns].astype(f32)
    out_ref[...] = total
    low_ref[...] = total.astype(bf16)


def summed(line, keep, far, at, wide):
    shape = (keep.shape[0], wide)
    return line.call(
        functools.partial(summed_kernel, at), "summed", [shaped(shape, f32), shaped(shape, bf16)]
    )(keep, far)


def joined_kernel(side, own, far, in_ref, out_ref, gain_ref):
    half = out_ref.shape[1] // 2
    on_side = side[0] == 0
    for at in range(4):
        columns = slice(at * half, (at + 1) * half)
        mine, theirs = own[:, columns], far[:, columns].astype(f32)
        target, start = (in_ref, 2 * at * half) if at < 3 else (out_ref, 0)
        target[:, start : start + half] = jnp.where(on_side, mine, theirs)
        target[:, start + half : start + 2 * half] = jnp.where(on_side, theirs, mine)
    both = own[:, 4 * half :] + far[:, 4 * half :].astype(f32)
    kind = lax.broadcasted_iota(jnp.int32, both.shape, 1)
    gain_ref[...] = jnp.where(kind == 0, both, own[:, 4 * half :])


def joined(line, side, own, far):
    count, wide = own.shape
    half = (wide - LANES) // 4
    return line.call(
        joined_kernel,
        "joined",
        [shaped((count, 6 * half), f32), shaped((count, 2 * half), f32), shaped((count, LANES), f32)],
        small=1,
        leaves=True,
    )(side, own, far)


def body(
    tokens,
    segment_ids,
    expert_ids,
    norm_first,
    project_in,
    project_out,
    norm_second,
    up_weight,
    down_weight,
    cotangent,
):
    own_count, width = tokens.shape[1], tokens.shape[2]
    side = lax.axis_index("blk").astype(jnp.int32)[None]
    count = lax.axis_size("dp")
    place = (lax.axis_index("dp") % INNER).astype(jnp.int32)[None]
    outer = count // INNER
    deep = width // count
    line = Line()

    own_tokens, own_grads = tokens[0], cotangent[0]
    far_tokens = across_blk(own_tokens)
    (
        bias, hot, hot_row, order, gains, own_rows, own_normed, own_cot, cot_sent, own_done,
        own_active, w_in, w_down, w_up, w_out,
    ) = begin(
        line, place, side, segment_ids, expert_ids, own_tokens, own_grads, norm_first, norm_second,
        (project_in, down_weight, up_weight, project_out), deep, outer,
    )
    far_cot = across_blk(cot_sent)
    rows = hot.shape[0]
    size = shortened(rows, own_count)
    mine, packed, middle, low_rows, lse = front(
        line, side, far_tokens, own_rows, own_normed, own_done, bias, gains, w_in, w_out
    )
    line.step = "active"
    sent, slope = up_forward(line, packed, hot, hot_row, own_cot, far_cot, w_up)
    sent_far = across_dp(sent, CORE)

    def over_outer(value, axis):
        if outer == 1:
            return value
        groups = [[o * INNER + i for o in range(outer)] for i in range(INNER)]
        return lax.psum_scatter(
            value, "dp", scatter_dimension=axis, tiled=True, axis_index_groups=groups
        )

    state, made, places = {}, {}, {}

    def send(name, axis, keep, going):
        state[name] = (keep, across_dp(going, axis))

    for step in STEPS:
        line.step = step
        if step[0] == "+":
            send(step[1:], PIECES[step[1:]][1][1], *added(line, [state[step[1:]]]))
        elif step[0] == "=":
            (group,) = [names for names in GROUPS if names[0] == step[1:]]
            at = 0
            for name in group:
                places[name] = (step, at)
                at += state[name][0].shape[1]
            send(step, FAR, *added(line, [state[name] for name in group]))
        elif step == "in":
            axis = PIECES[step][1][0]
            send(step, axis, *attention_grad(line, axis, order, sides, message, message_far))
        elif step in PIECES:
            (start, stop), (axis, _) = PIECES[step]
            pair = (later, later_far) if step[0] == "u" else (sent, sent_far)
            send(step, axis, *expert_grad(line, axis, made[step[0]], *pair, start * UNIT, stop * UNIT))
        elif step == "gu":
            (later,) = grad_upward_of(line, far_cot, packed, hot, w_down, slope, own_grad)
            later_far = across_dp(later, CORE)
        elif step == "half":
            own_grad, part_own = own_normed_of(line, own_active, slope, hot, w_up, size)
            far_own = across_blk(part_own)
        elif step == "rest":
            (part_rest,) = far_normed_of(line, later, hot, w_up, size)
            far_rest = across_blk(part_rest)
        elif step == "weights":
            (weights,) = weights_of(line, side, mine, lse, bias)
        elif step == "branch":
            branch, branch_send = branch_of(line, sent, hot, w_down, size)
            branch_far = across_blk(branch_send)
        elif step == "cot":
            made["d"] = picked_grads(line, order, hot_row, sent, sent_far)
        elif step == "two":
            made["u"] = picked(line, order, hot_row, sent_far, later, later_far)
        elif step == "pick":
            (sides,) = turned(line, order, later, later_far, rows)
        elif step == "back":
            message, gm_own, gn_own, gn_send = back(
                line, side, w_in, w_out, part_own, part_rest, far_own, far_rest, own_cot,
                far_cot, middle, low_rows, gains, mine, weights,
            )
            message_far = across_dp(message, CORE)
            gn_far = across_blk(gn_send)
        elif step == "last":
            input_grad, layer_out = last(
                line, gm_own, gn_own, gn_far, low_rows, gains, middle, branch, branch_far, own_count
            )
        elif step in ("down", "up"):
            names = sorted(n for n in PIECES if n[0] == step[0])
            groups = sorted({places[n][0] for n in names})
            cut = [
                (groups.index(places[n][0]), places[n][1], (PIECES[n][0][1] - PIECES[n][0][0]) * UNIT)
                for n in names
            ]
            made[step] = finished(line, [state[g] for g in groups], cut)
        elif step == "sum":
            wide = 2 * width + LANES
            in_sum, in_low = summed(line, *state[places["in"][0]], places["in"][1], wide)
            if outer > 1:
                in_sum = over_outer(in_sum, 0)
                in_low = in_sum.astype(bf16)
            in_far = across_blk(in_low)
        elif step == "join":
            in_out, out_out, gain_out = joined(line, side, in_sum, in_far)

    up_out = over_outer(made["up"], 1)
    down_out = over_outer(made["down"], 1).transpose(0, 2, 1)
    return (
        layer_out[None],
        input_grad[None],
        gain_out[:, 0],
        in_out,
        out_out,
        gain_out[:, 1],
        up_out,
        down_out,
    )


def solution(mesh):
    return jax.shard_map(
        body,
        mesh=mesh,
        in_specs=(
            P("dp", "blk", None),
            P("dp", None),
            P("dp", None),
            P(),
            P(),
            P(),
            P(),
            P(None, None, "blk"),
            P(None, "blk", None),
            P("dp", "blk", None),
        ),
        out_specs=(
            P("dp", "blk", None),
            P("dp", "blk", None),
            P("dp"),
            P("dp", None),
            P("dp", None),
            P("dp"),
            P(None, "dp", "blk"),
            P(None, "blk", "dp"),
        ),
        check_vma=False,
    )
```

```python
import functools

import jax
import jax.numpy as jnp
import numpy as np
from jax import lax
from jax.experimental import pallas as pl
from jax.experimental.pallas import tpu as pltpu
from jax.sharding import PartitionSpec as P

HEAD_DIM = 64
EXPERTS = 3
EPSILON = 1e-05
NEGATIVE = -1e30
ROOT_HALF = 0.7071067811865476
INV_ROOT_TAU = 0.3989422804014327
SCALE = HEAD_DIM ** (-0.5)
LOG2_E = 1.4426950408889634
LANES = 128
CHUNK = 512
UNIT = 256
INNER = 16
CORE, NEAR, MID, FAR = 1, 2, 4, 8
COSTS = {'down': 3, 'last': 60, 'half': 10}
HELD_BACK = {
    None: 1, "active": 2, "half": 6, "gu": 12, "cot": 13, "d0": 14, "d1": 18, "rest": 29, "two": 30,
    "pick": 31, "u3": 33, "weights": 34, "back": 36, "+d1": 36, "+d0": 36, "in": 37, "u2": 39, "branch": 42,
    "=d0": 42, "+u3": 48, "+in": 48, "u0": 50, "last": 51, "+u2": 51, "=in": 51, "u1": 54, "+u0": 54,
    "=u2": 54, "down": 54, "+u1": 54, "sum": 54, "=u0": 54, "join": 54, "=u1": 54, "up": 54,
}

PIECES = {
    "d0": ((0, 4), (MID, NEAR)),
    "d1": ((4, 6), (NEAR, MID)),
    "u0": ((0, 1), (NEAR, MID)),
    "u1": ((1, 2), (NEAR, MID)),
    "u2": ((2, 4), (NEAR, MID)),
    "u3": ((4, 6), (NEAR, MID)),
    "in": (None, (MID, NEAR)),
}
GROUPS = (("in",), ("d0", "d1"), ("u2", "u3"), ("u0",), ("u1",))
STEPS = (
    "half", "gu", "cot", "d0", "d1", "rest", "two", "pick", "u3", "weights", "back", "+d0", "+d1", "in", "u2",
    "branch", "=d0", "+u3", "+in", "u0", "last", "+u2", "=in", "u1", "+u0", "=u2", "down", "+u1", "sum", "=u0",
    "join", "=u1", "up",
)

f32 = jnp.float32
bf16 = jnp.bfloat16

NN = ((1,), (0,))
NT = ((1,), (1,))


def across_blk(value):
    return lax.ppermute(value, "blk", [(0, 1), (1, 0)])


def across_dp(value, bit):
    count = lax.axis_size("dp")
    return lax.ppermute(value, "dp", [(source, source ^ bit) for source in range(count)])


def dot(a, b, dims=NN):
    return lax.dot_general(a, b, (dims, ((), ())), preferred_element_type=f32)


def layer_norm_parts(values):
    row_mean = jnp.mean(values, axis=-1, keepdims=True)
    centred = values - row_mean
    row_var = jnp.mean(centred * centred, axis=-1, keepdims=True)
    scale = lax.rsqrt(row_var + EPSILON)
    return centred * scale, scale


def layer_norm_back(grad, gain, unit, scale):
    raised = grad * gain
    return scale * (
        raised
        - jnp.mean(raised, axis=-1, keepdims=True)
        - unit * jnp.mean(raised * unit, axis=-1, keepdims=True)
    )


def shaped(shape, dtype):
    return jax.ShapeDtypeStruct(shape, dtype)


def held(shape, dtype):
    size = np.dtype(dtype).itemsize
    shape = (1,) * (2 - len(shape)) + tuple(shape)
    lead = int(np.prod(shape[:-2])) if len(shape) > 2 else 1
    return lead * -(-shape[-2] // 16) * 16 * -(-shape[-1] // LANES) * LANES * size


class Line:
    def __init__(self):
        self.last, self.step = None, None

    def call(self, kernel, name, outs, scratch=(), small=0, large=0, room=3, leaves=False):
        def run(*operands):
            count, total = len(operands), len(outs)
            need = sum(held(v.shape, v.dtype) for v in scratch if v.memory_space == pltpu.VMEM)
            if leaves:
                need += sum(held(v.shape, v.dtype) for v in outs)
                results = list(outs)
            else:
                results = [pltpu.VMEM(v.shape, v.dtype) for v in outs]
            whole = pl.BlockSpec(memory_space=pltpu.VMEM)
            far = pl.BlockSpec(memory_space=pltpu.HBM)
            specs = [pl.BlockSpec(memory_space=pltpu.SMEM)] * small + [far] * large
            specs += [whole] * (count - small - large)
            places = [None] * small + [pltpu.HBM] * large + [pltpu.VMEM] * (count - small - large)
            operands = tuple(
                v if place is None else pltpu.with_memory_space_constraint(v, place)
                for v, place in zip(operands, places)
            )
            if self.last is not None:
                operands += (pltpu.with_memory_space_constraint(self.last, pltpu.HBM),)
                specs.append(far)
            first = len(operands)

            def body_of(*refs):
                kernel(*refs[:count], *refs[first : first + total], *refs[first + total + 1 :])

            *result, self.last = pl.pallas_call(
                body_of,
                name=name,
                out_shape=[*results, pltpu.HBM((HELD_BACK.get(self.step, HELD_BACK[None]) * 2048, LANES), f32)],
                in_specs=specs,
                out_specs=[whole] * total + [far],
                scratch_shapes=list(scratch),
                compiler_params=pltpu.CompilerParams(vmem_limit_bytes=need + room * 2**20),
                cost_estimate=pl.CostEstimate(
                    flops=COSTS.get(self.step, 10) * 10**9, bytes_accessed=1000, transcendentals=0
                ),
            )(*operands)
            return result

        return run


def masked_rows(target, value, hot):
    span = value.shape[1]
    for e in range(EXPERTS):
        target[:, e * span : (e + 1) * span] = value * hot[:, e : e + 1]


def grad_active_of(target, masked, weight):
    width, hidden = weight.shape[2], weight.shape[1]
    for n in range(0, hidden, CHUNK):
        total = dot(masked[:, :width], weight[0, n : n + CHUNK, :], NT)
        for e in range(1, EXPERTS):
            total += dot(masked[:, e * width : (e + 1) * width], weight[e, n : n + CHUNK, :], NT)
        target(slice(n, n + CHUNK), total)


def begin_kernel(
    deep, outer, place, side, ids_hbm, experts_hbm, tokens_hbm, grads_hbm, one_hbm, two_hbm,
    w_in_hbm, down_hbm, up_hbm, w_out_hbm,
    bias, hot, hot_row, order, gains, own_rows, own_normed, own_cot, cot_sent, projected,
    grad_active, w_in, down, up, w_out,
    ids, experts, tokens, grads, one, two, masked, sems,
):
    pairs = (
        (ids_hbm, ids), (experts_hbm, experts), (tokens_hbm, tokens), (one_hbm, one),
        (grads_hbm, grads), (two_hbm, two), (w_in_hbm, w_in), (down_hbm, down),
        (up_hbm, up), (w_out_hbm, w_out),
    )
    copies = [pltpu.make_async_copy(a, b, sems.at[at]) for at, (a, b) in enumerate(pairs)]
    for copy in copies:
        copy.start()
    rows, (count, width) = hot.shape[0], tokens.shape
    span = rows // 2
    on_side = side[0] == 0
    step = outer * deep
    lane = lax.broadcasted_iota(jnp.int32, (step, width), 1)
    low = lax.broadcasted_iota(jnp.int32, (step, width), 0)
    skip = low
    for late in range(1, outer):
        skip += jnp.where(low >= late * deep, (INNER - 1) * deep, 0)
    for block in range(INNER // 2):
        relative = ((block >> 2) & 1) * NEAR + ((block >> 1) & 1) * MID + (block & 1) * FAR
        base = (place[0] ^ relative) * deep
        order[block * step : (block + 1) * step, :] = (lane - base == skip).astype(f32).astype(bf16)
    for copy in copies[:6]:
        copy.wait()

    def both(values):
        halves = values[0:1, :count], values[0:1, count:]
        pad = jnp.full((1, span - count), -1, jnp.int32)
        first = jnp.where(on_side, halves[0], halves[1])
        second = jnp.where(on_side, halves[1], halves[0])
        return jnp.broadcast_to(jnp.concatenate([first, pad, second, pad], axis=1), (8, rows))

    segments, expert = both(ids), both(experts)
    keys = jnp.transpose(segments)[:, 0:1]
    bias[...] = jnp.where((keys == 0) | (keys == segments[0:1, :]), 0.0, NEGATIVE)
    hot_row[...] = (lax.broadcasted_iota(jnp.int32, (8, rows), 0) == expert).astype(f32)
    hot[...] = (lax.broadcasted_iota(jnp.int32, (rows, 8), 1) == jnp.transpose(expert)).astype(bf16)
    gains[...] = jnp.zeros_like(gains)
    gains[0:1, :] = one[...].reshape(1, width)
    gains[1:2, :] = two[...].reshape(1, width)
    own_cot[...] = jnp.zeros_like(own_cot)
    own_cot[0:count, :] = grads[...]
    cot_sent[...] = own_cot[: cot_sent.shape[0], :]
    own_rows[...] = jnp.zeros_like(own_rows)
    own_rows[0:count, :] = tokens[...]
    unit, _ = layer_norm_parts(own_rows[...].astype(f32))
    normed = (unit * gains[0:1, :]).astype(bf16)
    own_normed[...] = normed
    copies[6].wait()
    projected[...] = dot(normed, w_in[...]).astype(bf16)
    masked_rows(masked, own_cot[...], hot[:span, :])
    copies[7].wait()

    def store(columns, total):
        grad_active[:, columns] = total

    grad_active_of(store, masked, down)
    for copy in copies[8:]:
        copy.wait()


def begin(line, place, side, ids, experts, tokens, grads, one, two, weights, deep, outer):
    count, width = tokens.shape
    hidden = weights[1].shape[1]
    span = -(-count // LANES) * LANES
    rows = 2 * span
    inside = (ids, experts, tokens, grads, one, two)
    return line.call(
        functools.partial(begin_kernel, deep, outer),
        "begin",
        [
            shaped((rows, rows), f32),
            shaped((rows, 8), bf16),
            shaped((8, rows), f32),
            shaped((width // 2, width), bf16),
            shaped((8, width), f32),
            shaped((span, width), bf16),
            shaped((span, width), bf16),
            shaped((span, width), bf16),
            shaped((shortened(rows, count), width), bf16),
            shaped((span, 3 * width), bf16),
            shaped((span, hidden), f32),
            *[shaped(w.shape, w.dtype) for w in weights],
        ],
        scratch=[
            *[pltpu.VMEM(v.shape, v.dtype) for v in inside],
            pltpu.VMEM((span, EXPERTS * width), bf16),
            pltpu.SemaphoreType.DMA((10,)),
        ],
        small=2,
        large=10,
    )(place, side, *inside, *weights)


def front_kernel(
    side, far, own_rows, own_normed, own_done, bias, gains, w_in, w_out,
    mine_ref, packed, middle_ref, low_rows, lse_ref, projected,
):
    count, width = far.shape
    rows = projected.shape[0]
    span, own = rows // 2, width // 2
    low_rows[0:span, :] = own_rows[...]
    low_rows[span:, :] = jnp.zeros((span, width), bf16)
    low_rows[span : span + count, :] = far[...]
    unit, _ = layer_norm_parts(low_rows[span:, :].astype(f32))
    normed = (unit * gains[0:1, :]).astype(bf16)
    packed[1, :span, :] = own_normed[...]
    packed[1, span:, :] = normed
    projected[:span, :] = own_done[...]
    projected[span:, :] = dot(normed, w_in[...]).astype(bf16)
    first = lax.broadcasted_iota(jnp.int32, (rows, LANES), 1) < HEAD_DIM
    top = lax.broadcasted_iota(jnp.int32, (LANES, rows), 0) < HEAD_DIM
    lse_ref[...] = jnp.zeros_like(lse_ref)
    for p in range(width // LANES):
        columns = slice(p * LANES, (p + 1) * LANES)
        queries = projected[:, columns] * jnp.asarray(SCALE, bf16)
        keys = projected[:, width + p * LANES : width + (p + 1) * LANES]
        values = jnp.transpose(projected[:, 2 * width + p * LANES : 2 * width + (p + 1) * LANES])
        outs = []
        for head in range(2):
            mine, mine_up = (first, top) if head == 0 else (~first, ~top)
            scores = dot(keys, jnp.where(mine, queries, jnp.zeros_like(queries)), NT)
            scores = scores * LOG2_E + bias[...]
            peak = jnp.max(scores, axis=0, keepdims=True)
            raised = jnp.exp2(scores - peak).astype(bf16)
            summed = dot(jnp.where(mine_up, values, jnp.ones_like(values)), raised)
            at = (1 - head) * HEAD_DIM
            total = summed[at : at + 1, :]
            outs.append(summed * (1.0 / total))
            lse_ref[2 * p + head : 2 * p + head + 1, :] = peak + jnp.log2(total)
        packed[2, :, columns] = jnp.transpose(jnp.where(top, outs[0], outs[1])).astype(bf16)
    for at in range(3):
        start = pl.multiple_of(at * width + side[0] * own, LANES)
        mine_ref[:, at * own : (at + 1) * own] = projected[:, pl.ds(start, own)]
    middle = low_rows[...].astype(f32) + dot(packed[2], w_out[...])
    middle_ref[...] = middle
    unit, _ = layer_norm_parts(middle)
    packed[0] = (unit * gains[1:2, :]).astype(bf16)


def front(line, side, far, own_rows, own_normed, own_done, bias, gains, w_in, w_out):
    span, width = own_rows.shape
    rows = 2 * span
    return line.call(
        front_kernel,
        "front",
        [
            shaped((rows, 3 * width // 2), bf16),
            shaped((3, rows, width), bf16),
            shaped((rows, width), f32),
            shaped((rows, width), bf16),
            shaped((16, rows), f32),
        ],
        scratch=[pltpu.VMEM((rows, 3 * width), bf16)],
        small=1,
        room=5,
    )(side, far, own_rows, own_normed, own_done, bias, gains, w_in, w_out)


def plane(message, at, side):
    span = 2 * LANES
    width = message.shape[1] // 2
    start = (2 + at) * span
    return message.at[start : start + span, side * width : (side + 1) * width]


def up_kernel(packed, hot, hot_row, own_cot, far_cot, weight, message, slope_ref, masked):
    _, rows, width = packed.shape
    span, hidden = rows // 2, weight.shape[2]
    masked_rows(masked, packed[0], hot)
    message[:span, hidden:] = own_cot[...]
    sent = far_cot.shape[0]
    message[span : span + sent, hidden:] = far_cot[...]
    message[span + sent : rows, hidden:] = jnp.zeros((span - sent, width), bf16)
    message[rows:, :] = jnp.zeros_like(message[rows:, :])
    message[rows : rows + 8, :rows] = hot_row[...].astype(bf16)
    for n in range(0, hidden, CHUNK):
        part = weight[:, :, n : n + CHUNK].reshape(EXPERTS * width, CHUNK)
        upward = dot(masked[...], part)
        half = 0.5 * (1.0 + lax.erf(upward * ROOT_HALF))
        message[:rows, n : n + CHUNK] = (upward * half).astype(bf16)
        slope_ref[:, n : n + CHUNK] = half + upward * INV_ROOT_TAU * jnp.exp(-0.5 * upward * upward)


def up_forward(line, packed, hot, hot_row, own_cot, far_cot, weight):
    _, rows, width = packed.shape
    hidden = weight.shape[2]
    return line.call(
        up_kernel,
        "up_forward",
        [shaped((rows + 16, hidden + width), bf16), shaped((rows, hidden), f32)],
        scratch=[pltpu.VMEM((rows, EXPERTS * width), bf16)],
        room=5,
    )(packed, hot, hot_row, own_cot, far_cot, weight)


def grad_upward_kernel(far_cot, packed, hot, weight, slope, own_grad, out_ref, masked):
    rows = hot.shape[0]
    span = rows // 2
    sent = far_cot.shape[0]
    masked[sent:, :] = jnp.zeros_like(masked[sent:, :])
    masked_rows(masked.at[:sent, :], far_cot[...], hot[span : span + sent, :])
    for half in range(2):
        for at in range(3):
            plane(out_ref, at, half)[...] = packed[at, half * span : (half + 1) * span, :]

    def store(columns, total):
        out_ref[:span, columns] = own_grad[:, columns]
        out_ref[span:rows, columns] = (total * slope[span:, columns]).astype(bf16)

    grad_active_of(store, masked, weight)


def grad_upward_of(line, far_cot, packed, hot, weight, slope, own_grad):
    _, rows, width = packed.shape
    hidden = weight.shape[1]
    return line.call(
        grad_upward_kernel,
        "grad_upward",
        [shaped((5 * rows // 2, hidden), bf16)],
        scratch=[pltpu.VMEM((rows // 2, EXPERTS * width), bf16)],
        room=5,
    )(far_cot, packed, hot, weight, slope, own_grad)


def shortened(rows, count):
    return min(rows // 2, -(-count // 16) * 16)


def half_normed(masked, weight, out_ref):
    hidden, size, wide = weight.shape[2], out_ref.shape[0], 256
    for n in range(0, out_ref.shape[1], wide):
        total = dot(masked[:, :hidden], weight[0, n : n + wide, :], NT)
        for e in range(1, EXPERTS):
            total += dot(masked[:, e * hidden : (e + 1) * hidden], weight[e, n : n + wide, :], NT)
        out_ref[:, n : n + wide] = total[:size].astype(bf16)


def own_normed_kernel(own_active, slope, hot, weight, grad_ref, out_ref, masked):
    span = own_active.shape[0]
    grad_ref[...] = (own_active[...] * slope[:span, :]).astype(bf16)
    masked_rows(masked, grad_ref[...], hot[:span, :])
    half_normed(masked, weight, out_ref)


def own_normed_of(line, own_active, slope, hot, weight, size):
    span, hidden = own_active.shape
    return line.call(
        own_normed_kernel,
        "own_normed",
        [shaped((span, hidden), bf16), shaped((size, weight.shape[1]), bf16)],
        scratch=[pltpu.VMEM((span, EXPERTS * hidden), bf16)],
        room=5,
    )(own_active, slope, hot, weight)


def far_normed_kernel(message, hot, weight, out_ref, masked):
    rows = hot.shape[0]
    masked_rows(masked, message[rows // 2 : rows, :], hot[rows // 2 :, :])
    half_normed(masked, weight, out_ref)


def far_normed_of(line, message, hot, weight, size):
    rows, hidden = hot.shape[0], weight.shape[2]
    return line.call(
        far_normed_kernel,
        "far_normed",
        [shaped((size, weight.shape[1]), bf16)],
        scratch=[pltpu.VMEM((rows // 2, EXPERTS * hidden), bf16)],
        room=5,
    )(message, hot, weight)


def branch_kernel(sent, hot, weight, own_ref, send_ref, masked):
    rows, hidden = hot.shape[0], weight.shape[1]
    size, width = own_ref.shape
    masked_rows(masked, sent[:rows, :hidden], hot)
    wide = 256
    for n in range(0, width, wide):
        columns = slice(n, n + wide)
        total = dot(masked[:, :hidden], weight[0, :, columns])
        for e in range(1, EXPERTS):
            total += dot(masked[:, e * hidden : (e + 1) * hidden], weight[e, :, columns])
        own_ref[:, columns] = total[:size].astype(bf16)
        send_ref[:, columns] = total[rows // 2 : rows // 2 + size].astype(bf16)


def branch_of(line, sent, hot, weight, size):
    rows, (_, hidden, width) = hot.shape[0], weight.shape
    shape = shaped((size, width), bf16)
    return line.call(
        branch_kernel,
        "branch",
        [shape, shape],
        scratch=[pltpu.VMEM((rows, EXPERTS * hidden), bf16)],
        room=5,
    )(sent, hot, weight)


def masked_turned(order, rows, hot, target, part):
    turned = dot(order[...], rows, NT)
    for e in range(EXPERTS):
        target[e, :, part] = (turned * hot[e : e + 1, part].astype(f32)).astype(bf16)


def picked_grads_kernel(order, hot_own, own, far, own_ref, far_ref):
    rows, width = own_ref.shape[2], order.shape[1]
    hidden = own.shape[1] - width
    every = slice(0, rows)
    masked_turned(order, own[:rows, hidden:], hot_own, own_ref, every)
    masked_turned(order, far[:rows, hidden:], far.at[rows:, :], far_ref, every)


def picked_grads(line, order, hot_own, own, far):
    shape = shaped((EXPERTS, order.shape[0], hot_own.shape[1]), bf16)
    return line.call(picked_grads_kernel, "picked", [shape, shape])(order, hot_own, own, far)


def picked_kernel(order, hot_own, first, own, far, own_ref, far_ref):
    rows = own_ref.shape[2]
    span = rows // 2
    for source, hot, target in ((own, hot_own, own_ref), (far, first.at[rows:, :], far_ref)):
        for half in range(2):
            part = slice(half * span, (half + 1) * span)
            masked_turned(order, plane(source, 0, half)[...], hot, target, part)


def picked(line, order, hot_own, first, own, far):
    shape = shaped((EXPERTS, order.shape[0], hot_own.shape[1]), bf16)
    return line.call(picked_kernel, "picked", [shape, shape])(order, hot_own, first, own, far)


def turned_kernel(order, own, far, out_ref):
    span = out_ref.shape[2] // 2
    for at, (source, part) in enumerate(((own, 1), (far, 1), (own, 2), (far, 2))):
        for half in range(2):
            turned = dot(order[...], plane(source, part, half)[...], NT)
            out_ref[at, :, half * span : (half + 1) * span] = turned.astype(bf16)


def turned(line, order, own, far, rows):
    shape = shaped((4, order.shape[0], rows), bf16)
    return line.call(turned_kernel, "turned", [shape])(order, own, far)


def split_store(first, value, columns, keep_ref, send_ref):
    value = value.astype(bf16)
    half, quarter = value.shape[0] // 2, value.shape[0] // 4
    if first == NEAR:
        keep_ref[:, columns] = value[:half]
        send_ref[:, columns] = value[half:]
    else:
        for part in range(2):
            rows = slice(part * quarter, (part + 1) * quarter)
            keep_ref[rows, columns] = value[part * half : part * half + quarter]
            send_ref[rows, columns] = value[part * half + quarter : (part + 1) * half]


def expert_grad_kernel(first, start, stop, a_own, a_far, own, far, keep_ref, send_ref):
    rows = a_own.shape[2]
    for n in range(start, stop, CHUNK):
        wide = min(CHUNK, stop - n)
        for e in range(EXPERTS):
            both = dot(a_own[e], own[:rows, n : n + wide]) + dot(a_far[e], far[:rows, n : n + wide])
            at = e * (stop - start) + n - start
            split_store(first, both, slice(at, at + wide), keep_ref, send_ref)


def expert_grad(line, first, sides, own, far, start, stop):
    shape = shaped((sides[0].shape[1] // 2, EXPERTS * (stop - start)), bf16)
    return line.call(
        functools.partial(expert_grad_kernel, first, start, stop),
        "expert_grad",
        [shape, shape],
        room=4,
    )(*sides, own, far)


def attention_grad_kernel(first, order, sides, g_own, g_far, keep_ref, send_ref):
    rows, span = sides.shape[2], g_own.shape[1]
    for at in range(4):
        part = slice(at * rows, (at + 1) * rows)
        pair = 0 if at < 3 else 2
        both = dot(sides[pair], g_own[part, :]) + dot(sides[pair + 1], g_far[part, :])
        split_store(first, both, slice(at * span, (at + 1) * span), keep_ref, send_ref)
    sums = g_own[4 * rows : 4 * rows + 16, :].astype(f32)
    sums += g_far[4 * rows : 4 * rows + 16, :].astype(f32)
    both = dot(order[:, :span], sums[0:8].astype(bf16), NT)
    both += dot(order[:, span:], sums[8:16].astype(bf16), NT)
    tail = jnp.concatenate([both, jnp.zeros((both.shape[0], LANES - 8), f32)], axis=1)
    split_store(first, tail, slice(4 * span, 4 * span + LANES), keep_ref, send_ref)


def attention_grad(line, first, order, sides, g_own, g_far):
    shape = shaped((order.shape[0] // 2, 4 * g_own.shape[1] + LANES), bf16)
    return line.call(
        functools.partial(attention_grad_kernel, first), "attention_grad", [shape, shape]
    )(order, sides, g_own, g_far)


def weights_kernel(side, mine_ref, lse, bias, out_ref):
    rows, own = mine_ref.shape[0], mine_ref.shape[1] // 3
    first = lax.broadcasted_iota(jnp.int32, (rows, LANES), 1) < HEAD_DIM
    on_side = side[0] == 0
    for at in range(own // HEAD_DIM):
        columns = slice(at // 2 * LANES, (at // 2 + 1) * LANES)
        queries = mine_ref[:, columns] * jnp.asarray(SCALE, bf16)
        keys = mine_ref[:, own + at // 2 * LANES : own + (at // 2 + 1) * LANES]
        mine = first if at % 2 == 0 else ~first
        far_at = at + own // HEAD_DIM
        lse_row = jnp.where(on_side, lse[at : at + 1, :], lse[far_at : far_at + 1, :])
        scores = dot(keys, jnp.where(mine, queries, jnp.zeros_like(queries)), NT) * LOG2_E
        out_ref[at] = jnp.exp2(scores + bias[...] - lse_row).astype(bf16)


def weights_of(line, side, mine, lse, bias):
    rows, three = mine.shape
    return line.call(
        weights_kernel,
        "weights",
        [shaped((three // 3 // HEAD_DIM, rows, rows), bf16)],
        small=1,
        room=5,
    )(side, mine, lse, bias)


def back_kernel(
    side, w_in, w_out, part_own, part_rest, far_own, far_rest, own_cot, far_cot, middle, low_rows, gains,
    mine_ref, weights, message, gm_ref, gn_ref, gn_send, branch_low, attended_back,
):
    rows, width = middle.shape
    span, own = rows // 2, width // 2
    size = gn_send.shape[0]
    start = side[0] * own
    unit, scale = layer_norm_parts(middle[...])
    blank = jnp.zeros((span - size, width), f32)
    first = part_own[...].astype(f32) + far_rest[...].astype(f32)
    second = part_rest[...].astype(f32) + far_own[...].astype(f32)
    grad = jnp.concatenate([first, blank, second, blank], axis=0)
    gains_two = jnp.sum(grad * unit, axis=0, keepdims=True)
    blank = jnp.zeros((span - size, width), bf16)
    grads_low = jnp.concatenate([own_cot[...], far_cot[...], blank], axis=0)
    grad_middle = grads_low.astype(f32) + layer_norm_back(grad, gains[1:2, :], unit, scale)
    gm_ref[...] = grad_middle[:span]
    branch_low[...] = grad_middle.astype(bf16)
    out_rows = pl.ds(pl.multiple_of(start, LANES), own)
    attended_back[...] = dot(branch_low[...], w_out[out_rows, :], NT).astype(bf16)
    first = lax.broadcasted_iota(jnp.int32, (rows, LANES), 1) < HEAD_DIM
    top = lax.broadcasted_iota(jnp.int32, (LANES, rows), 0) < HEAD_DIM
    for p in range(own // LANES):
        columns = slice(p * LANES, (p + 1) * LANES)
        queries = mine_ref[:, columns] * jnp.asarray(SCALE, bf16)
        keys = mine_ref[:, own + p * LANES : own + (p + 1) * LANES]
        values = mine_ref[:, 2 * own + p * LANES : 2 * own + (p + 1) * LANES]
        grads = attended_back[:, columns]
        keys_up = jnp.transpose(keys)
        parts = []
        for head in range(2):
            mine = first if head == 0 else jnp.logical_not(first)
            low_probs = weights[2 * p + head]
            probs = low_probs.astype(f32)
            dprobs = dot(values, jnp.where(mine, grads, jnp.zeros_like(grads)), NT)
            delta = jnp.sum(probs * dprobs, axis=0, keepdims=True)
            dscores = (probs * (dprobs - delta)).astype(bf16)
            parts.append(
                (
                    dot(keys_up, dscores) * SCALE,
                    dot(dscores, queries),
                    dot(low_probs, grads),
                )
            )
        turned_back = jnp.where(top, parts[0][0], parts[1][0])
        message[0:rows, columns] = jnp.transpose(turned_back).astype(bf16)
        for at in range(1, 3):
            message[at * rows : (at + 1) * rows, columns] = jnp.where(
                first, parts[0][at], parts[1][at]
            ).astype(bf16)
    message[3 * rows : 4 * rows, :] = branch_low[:, pl.ds(pl.multiple_of(start, LANES), own)]
    grad_normed = jnp.zeros((rows, width), f32)
    for at in range(3):
        columns = pl.ds(pl.multiple_of(at * width + start, LANES), own)
        grad_normed += dot(message[at * rows : (at + 1) * rows, :], w_in[:, columns], NT)
    gn_ref[...] = grad_normed[:span]
    gn_send[...] = grad_normed[span : span + size].astype(bf16)
    unit, _ = layer_norm_parts(low_rows[...].astype(f32))
    gains_one = jnp.sum(grad_normed * unit, axis=0, keepdims=True)
    blank = jnp.zeros((6, own), f32)
    message[4 * rows :, :] = jnp.concatenate(
        [
            gains_one[:, :own], gains_two[:, :own], blank,
            gains_one[:, own:], gains_two[:, own:], blank,
        ],
        axis=0,
    ).astype(bf16)


def back(
    line, side, w_in, w_out, part_own, part_rest, far_own, far_rest, own_cot, far_cot, middle, low_rows, gains,
    mine, weights,
):
    rows, width = middle.shape
    own, span, size = width // 2, rows // 2, part_own.shape[0]
    return line.call(
        back_kernel,
        "back",
        [
            shaped((4 * rows + 16, own), bf16),
            shaped((span, width), f32),
            shaped((span, width), f32),
            shaped((size, width), bf16),
        ],
        scratch=[
            pltpu.VMEM((rows, width), bf16),
            pltpu.VMEM((rows, own), bf16),
        ],
        small=1,
        room=7,
    )(
        side, w_in, w_out, part_own, part_rest, far_own, far_rest, own_cot, far_cot, middle, low_rows, gains,
        mine, weights,
    )


def last_kernel(gm, gn, gn_far, low_rows, gains, middle, branch, branch_far, out_ref, layer_ref):
    count, size = out_ref.shape[0], gn_far.shape[0]
    unit, scale = layer_norm_parts(low_rows[:size, :].astype(f32))
    grad = gn[:size, :] + gn_far[...].astype(f32)
    total = gm[:size, :] + layer_norm_back(grad, gains[0:1, :], unit, scale)
    out_ref[...] = total[:count].astype(bf16)
    total = middle[:size, :] + branch[...].astype(f32) + branch_far[...].astype(f32)
    layer_ref[...] = total[:count].astype(bf16)


def last(line, gm, gn, gn_far, low_rows, gains, middle, branch, branch_far, count):
    shape = shaped((count, gm.shape[1]), bf16)
    return line.call(last_kernel, "last", [shape, shape], leaves=True)(
        gm, gn, gn_far, low_rows, gains, middle, branch, branch_far
    )


def add_kernel(*refs):
    keep_ref, send_ref = refs[-2:]
    half, at = keep_ref.shape[0], 0
    for keep, far in zip(refs[0:-2:2], refs[1:-2:2]):
        columns = slice(at, at + keep.shape[1])
        total = keep[...].astype(f32) + far[...].astype(f32)
        keep_ref[:, columns] = total[:half].astype(bf16)
        send_ref[:, columns] = total[half:].astype(bf16)
        at += keep.shape[1]


def added(line, pairs):
    count, wide = pairs[0][0].shape[0], sum(pair[0].shape[1] for pair in pairs)
    shape = shaped((count // 2, wide), bf16)
    return line.call(add_kernel, "added", [shape, shape])(*[v for pair in pairs for v in pair])


def finish_kernel(places, *refs):
    out_ref, start = refs[-1], 0
    for (pair, at, wide) in places:
        keep, far = refs[2 * pair], refs[2 * pair + 1]
        for e in range(EXPERTS):
            columns = slice(at + e * wide, at + (e + 1) * wide)
            out_ref[e, :, start : start + wide] = keep[:, columns].astype(f32) + far[:, columns].astype(f32)
        start += wide


def finished(line, pairs, places):
    shape = (EXPERTS, pairs[0][0].shape[0], sum(place[2] for place in places))
    kernel = functools.partial(finish_kernel, places)
    return line.call(kernel, "finished", [shaped(shape, f32)], leaves=True)(
        *[v for pair in pairs for v in pair]
    )[0]


def summed_kernel(at, keep, far, out_ref, low_ref):
    columns = slice(at, at + out_ref.shape[1])
    total = keep[:, columns].astype(f32) + far[:, columns].astype(f32)
    out_ref[...] = total
    low_ref[...] = total.astype(bf16)


def summed(line, keep, far, at, wide):
    shape = (keep.shape[0], wide)
    return line.call(
        functools.partial(summed_kernel, at), "summed", [shaped(shape, f32), shaped(shape, bf16)]
    )(keep, far)


def joined_kernel(side, own, far, in_ref, out_ref, gain_ref):
    half = out_ref.shape[1] // 2
    on_side = side[0] == 0
    for at in range(4):
        columns = slice(at * half, (at + 1) * half)
        mine, theirs = own[:, columns], far[:, columns].astype(f32)
        target, start = (in_ref, 2 * at * half) if at < 3 else (out_ref, 0)
        target[:, start : start + half] = jnp.where(on_side, mine, theirs)
        target[:, start + half : start + 2 * half] = jnp.where(on_side, theirs, mine)
    both = own[:, 4 * half :] + far[:, 4 * half :].astype(f32)
    kind = lax.broadcasted_iota(jnp.int32, both.shape, 1)
    gain_ref[...] = jnp.where(kind == 0, both, own[:, 4 * half :])


def joined(line, side, own, far):
    count, wide = own.shape
    half = (wide - LANES) // 4
    return line.call(
        joined_kernel,
        "joined",
        [shaped((count, 6 * half), f32), shaped((count, 2 * half), f32), shaped((count, LANES), f32)],
        small=1,
        leaves=True,
    )(side, own, far)


def body(
    tokens,
    segment_ids,
    expert_ids,
    norm_first,
    project_in,
    project_out,
    norm_second,
    up_weight,
    down_weight,
    cotangent,
):
    own_count, width = tokens.shape[1], tokens.shape[2]
    side = lax.axis_index("blk").astype(jnp.int32)[None]
    count = lax.axis_size("dp")
    place = (lax.axis_index("dp") % INNER).astype(jnp.int32)[None]
    outer = count // INNER
    deep = width // count
    line = Line()

    own_tokens, own_grads = tokens[0], cotangent[0]
    far_tokens = across_blk(own_tokens)
    (
        bias, hot, hot_row, order, gains, own_rows, own_normed, own_cot, cot_sent, own_done,
        own_active, w_in, w_down, w_up, w_out,
    ) = begin(
        line, place, side, segment_ids, expert_ids, own_tokens, own_grads, norm_first, norm_second,
        (project_in, down_weight, up_weight, project_out), deep, outer,
    )
    far_cot = across_blk(cot_sent)
    rows = hot.shape[0]
    size = shortened(rows, own_count)
    mine, packed, middle, low_rows, lse = front(
        line, side, far_tokens, own_rows, own_normed, own_done, bias, gains, w_in, w_out
    )
    line.step = "active"
    sent, slope = up_forward(line, packed, hot, hot_row, own_cot, far_cot, w_up)
    sent_far = across_dp(sent, CORE)

    def over_outer(value, axis):
        if outer == 1:
            return value
        groups = [[o * INNER + i for o in range(outer)] for i in range(INNER)]
        return lax.psum_scatter(
            value, "dp", scatter_dimension=axis, tiled=True, axis_index_groups=groups
        )

    state, made, places = {}, {}, {}

    def send(name, axis, keep, going):
        state[name] = (keep, across_dp(going, axis))

    for step in STEPS:
        line.step = step
        if step[0] == "+":
            send(step[1:], PIECES[step[1:]][1][1], *added(line, [state[step[1:]]]))
        elif step[0] == "=":
            (group,) = [names for names in GROUPS if names[0] == step[1:]]
            at = 0
            for name in group:
                places[name] = (step, at)
                at += state[name][0].shape[1]
            send(step, FAR, *added(line, [state[name] for name in group]))
        elif step == "in":
            axis = PIECES[step][1][0]
            send(step, axis, *attention_grad(line, axis, order, sides, message, message_far))
        elif step in PIECES:
            (start, stop), (axis, _) = PIECES[step]
            pair = (later, later_far) if step[0] == "u" else (sent, sent_far)
            send(step, axis, *expert_grad(line, axis, made[step[0]], *pair, start * UNIT, stop * UNIT))
        elif step == "gu":
            (later,) = grad_upward_of(line, far_cot, packed, hot, w_down, slope, own_grad)
            later_far = across_dp(later, CORE)
        elif step == "half":
            own_grad, part_own = own_normed_of(line, own_active, slope, hot, w_up, size)
            far_own = across_blk(part_own)
        elif step == "rest":
            (part_rest,) = far_normed_of(line, later, hot, w_up, size)
            far_rest = across_blk(part_rest)
        elif step == "weights":
            (weights,) = weights_of(line, side, mine, lse, bias)
        elif step == "branch":
            branch, branch_send = branch_of(line, sent, hot, w_down, size)
            branch_far = across_blk(branch_send)
        elif step == "cot":
            made["d"] = picked_grads(line, order, hot_row, sent, sent_far)
        elif step == "two":
            made["u"] = picked(line, order, hot_row, sent_far, later, later_far)
        elif step == "pick":
            (sides,) = turned(line, order, later, later_far, rows)
        elif step == "back":
            message, gm_own, gn_own, gn_send = back(
                line, side, w_in, w_out, part_own, part_rest, far_own, far_rest, own_cot,
                far_cot, middle, low_rows, gains, mine, weights,
            )
            message_far = across_dp(message, CORE)
            gn_far = across_blk(gn_send)
        elif step == "last":
            input_grad, layer_out = last(
                line, gm_own, gn_own, gn_far, low_rows, gains, middle, branch, branch_far, own_count
            )
        elif step in ("down", "up"):
            names = sorted(n for n in PIECES if n[0] == step[0])
            groups = sorted({places[n][0] for n in names})
            cut = [
                (groups.index(places[n][0]), places[n][1], (PIECES[n][0][1] - PIECES[n][0][0]) * UNIT)
                for n in names
            ]
            made[step] = finished(line, [state[g] for g in groups], cut)
        elif step == "sum":
            wide = 2 * width + LANES
            in_sum, in_low = summed(line, *state[places["in"][0]], places["in"][1], wide)
            if outer > 1:
                in_sum = over_outer(in_sum, 0)
                in_low = in_sum.astype(bf16)
            in_far = across_blk(in_low)
        elif step == "join":
            in_out, out_out, gain_out = joined(line, side, in_sum, in_far)

    up_out = over_outer(made["up"], 1)
    down_out = over_outer(made["down"], 1).transpose(0, 2, 1)
    return (
        layer_out[None],
        input_grad[None],
        gain_out[:, 0],
        in_out,
        out_out,
        gain_out[:, 1],
        up_out,
        down_out,
    )


def solution(mesh):
    return jax.shard_map(
        body,
        mesh=mesh,
        in_specs=(
            P("dp", "blk", None),
            P("dp", None),
            P("dp", None),
            P(),
            P(),
            P(),
            P(),
            P(None, None, "blk"),
            P(None, "blk", None),
            P("dp", "blk", None),
        ),
        out_specs=(
            P("dp", "blk", None),
            P("dp", "blk", None),
            P("dp"),
            P("dp", None),
            P("dp", None),
            P("dp"),
            P(None, "dp", "blk"),
            P(None, "blk", "dp"),
        ),
        check_vma=False,
    )
```
